512 devices in a mesh: seg: 32 (over z, x_hi, core), patch: 16 (over x_lo, y).
Axes of the slice: x: 4 (x_hi: 2, x_lo: 2; x = x_hi * 2 + x_lo), y: 8, z: 8, core: 2. Of those that a mesh axis runs over, the one named last changes fastest.
Arguments:
- incident: bfloat16 [32, 64, 4096], P('seg', None, 'patch'), may hold values from -6 to 6
- wall_axial: float32 [32, 4096], P('seg'), may hold values from 0 to 1
- wall_angle: float32 [32, 4096], P('seg'), may hold values from -3.140625 to 3.140625
- wall_area: float32 [32, 4096], P('seg'), may hold values from 0.5 to 2
- visibility: int32 [32, 2, 32, 32], P('seg', None, 'patch'), may hold values 0 or 1
- end_reflection: float32 [2, 32], replicated, may hold values from -0.9 to 0.9
Outputs:
- currents: bfloat16 [32, 64, 4096], P('seg', None, 'patch')
The draws below stay inside these ranges and needn't reach their ends.
Inputs may be any that keep to these rules, and one draw needn't show every extreme that they name: `visibility`: 1 where the source block is lit for the target block, 0 where it is in shadow.
All inputs are finite; a program needn't handle non-finite values.
Results may differ from the reference program's by a relative error of at most 0.0034.
Values may be sent and summed in bfloat16 or wider, within the bound.
A program may use at most 64 MiB of HBM per device.

```python
import math
import jax
import jax.numpy as jnp
from jax import lax

PATCHES = 4096
ANGLES = 16
BLK = 128
ITERS = 2
NSEG = 32


def place_ends(values, key, low, top_value):
    spot = [jax.random.randint(jax.random.fold_in(key, axis), (), 0, length) for axis, length in enumerate(values.shape)]
    main_axis = values.shape.index(max(values.shape))
    neighbour = spot[:main_axis] + [(spot[main_axis] + 1) % values.shape[main_axis]] + spot[main_axis + 1:]
    return values.at[tuple(spot)].set(low).at[tuple(neighbour)].set(top_value)


def steps_of(rng, shape, cuts, low, largest):
    level, own = 1.0, jax.random.fold_in(rng, 6)
    for dim, parts in cuts:
        heights = jnp.exp(jax.random.uniform(jax.random.fold_in(own, dim), (parts,), jnp.float32, low / len(cuts), largest / len(cuts)))
        level = level * jnp.repeat(heights, shape[dim] // parts).reshape([-1 if axis == dim else 1 for axis in range(len(shape))])
    return level


def scatter_about(key, extent, scale, bound, pieces=(), kind=jnp.bfloat16):
    factor_of = steps_of(key, extent, pieces, -0.22, 0.18) if pieces else 1.0
    drawn = jax.random.normal(key, extent, jnp.float32) * scale * factor_of
    return jnp.minimum(jnp.maximum(drawn, -bound), bound).astype(kind)


def setup_inputs(seed: int = 0) -> dict:
    streams_of = jax.random.split(jax.random.key(seed), 7)
    return {
        "incident": scatter_about(streams_of[0], (NSEG, 4 * ANGLES, PATCHES), 1.0, 6.0, ((0, 32), (2, 16))),
        "wall_axial": jnp.clip(1.0 * jax.random.uniform(streams_of[1], (NSEG, PATCHES), jnp.float32) ** steps_of(streams_of[1], (NSEG, PATCHES), ((0, 32),), -0.2, 0.2), 0.0, 1.0),
        "wall_angle": jnp.clip(jax.random.uniform(streams_of[2], (NSEG, PATCHES), jnp.float32, -3.140625, 3.140625), -3.140625, 3.140625),
        "wall_area": jnp.clip(jnp.exp(math.log(2.0) - 1.3862944 * jax.random.uniform(streams_of[3], (NSEG, PATCHES), jnp.float32) ** steps_of(streams_of[3], (NSEG, PATCHES), ((0, 32),), -0.2, 0.2)), 0.5, 2.0),
        "visibility": place_ends((jax.random.randint(streams_of[4], (NSEG, 2, PATCHES // BLK, PATCHES // BLK), 0, 4) < 3).astype(jnp.int32), jax.random.fold_in(streams_of[4], 1), 0, 1),
        "end_reflection": jnp.clip(jax.random.uniform(streams_of[5], (2, 2 * ANGLES), jnp.float32, -0.9, 0.9), -0.9, 0.9),
    }


WAVENUMBER = 40.0
RADIUS = 0.5
SOFTENING = 0.25

def kernel_piece(target, source, offset, visible, patches):
    axial_gap = offset + target[0][:, None] - source[0][None, :]
    chord = 2.0 * RADIUS * RADIUS * (1.0 - jnp.cos(target[1][:, None] - source[1][None, :]))
    squared = axial_gap * axial_gap + chord
    magnitude = source[2][None, :] * visible.astype(jnp.float32) / jnp.sqrt(patches * (squared + SOFTENING))
    phases = WAVENUMBER * jnp.sqrt(squared)
    kernel_re = (magnitude * jnp.cos(phases)).astype(jnp.bfloat16)
    kernel_im = (-magnitude * jnp.sin(phases)).astype(jnp.bfloat16)
    return (kernel_re, kernel_im)

def couple(sources, kernel_re, kernel_im, angles):
    contract = (((1,), (1,)), ((), ()))
    prod_re = lax.dot_general(sources, kernel_re, contract, preferred_element_type=jnp.float32)
    prod_im = lax.dot_general(sources, kernel_im, contract, preferred_element_type=jnp.float32)
    return jnp.concatenate([prod_re[:angles] - prod_im[angles:], prod_re[angles:] + prod_im[:angles]], 0)

def reflect(coef, values, angles):
    coef_re = coef[:angles][:, None]
    coef_im = coef[angles:][:, None]
    real_part = values[:angles]
    imag_part = values[angles:]
    return jnp.concatenate([coef_re * real_part - coef_im * imag_part, coef_re * imag_part + coef_im * real_part], 0)

def reference(incident, wall_axial, wall_angle, wall_area, visibility, end_reflection):
    seg_count, channel_count, patches = incident.shape
    angles = channel_count // 4
    block_rows = min(1024, patches)
    block_count = patches // block_rows
    block_size = patches // visibility.shape[3]
    geometry = jnp.stack([wall_axial, wall_angle, wall_area], 1)
    empty_geometry = jnp.zeros((1, 3, patches), jnp.float32)
    prev_geo = jnp.concatenate([empty_geometry, geometry[:-1]], 0)
    next_geo = jnp.concatenate([geometry[1:], empty_geometry], 0)
    empty_currents = jnp.zeros((1, 2 * angles, patches), jnp.bfloat16)
    state = incident
    for sweep in range(ITERS):
        prev_cur = jnp.concatenate([empty_currents, state[:-1, :2 * angles]], 0)
        next_cur = jnp.concatenate([state[1:, 2 * angles:], empty_currents], 0)

        def one_segment(members):
            target_geo, before_geo, after_geo, before_cur, after_cur, visible = members

            def one_block(block_index):
                target = lax.dynamic_slice_in_dim(target_geo, block_index * block_rows, block_rows, 1)
                lit = lax.dynamic_slice_in_dim(visible, block_index * (block_rows // block_size), block_rows // block_size, 1)
                lit = jnp.repeat(jnp.repeat(lit, block_size, axis=1), block_size, axis=2)
                kernel_re, kernel_im = kernel_piece(target, before_geo, 1.0, lit[0], patches)
                forward = couple(before_cur, kernel_re, kernel_im, angles)
                kernel_re, kernel_im = kernel_piece(target, after_geo, -1.0, lit[1], patches)
                backward = couple(after_cur, kernel_re, kernel_im, angles)
                return jnp.concatenate([forward, backward], 0)
            result = lax.map(one_block, jnp.arange(block_count, dtype=jnp.int32))
            return jnp.transpose(result, (1, 0, 2)).reshape(channel_count, patches)
        coupled = lax.map(one_segment, (geometry, prev_geo, next_geo, prev_cur, next_cur, visibility))
        previous = state.astype(jnp.float32)
        first_end = reflect(end_reflection[0], previous[0, 2 * angles:], angles)
        last_end = reflect(end_reflection[1], previous[-1, :2 * angles], angles)
        mirrored = jnp.zeros((seg_count, channel_count, patches), jnp.float32)
        mirrored = mirrored.at[0, :2 * angles].set(first_end).at[seg_count - 1, 2 * angles:].set(last_end)
        state = (incident.astype(jnp.float32) + coupled + mirrored).astype(jnp.bfloat16)
    return state
```

```python
import functools
import math

import jax
import jax.numpy as jnp
from jax import lax
from jax.experimental import pallas as pl
from jax.experimental.pallas import tpu as pltpu
from jax.sharding import PartitionSpec as P

ITERS = 2
WAVENUMBER = 40.0
RADIUS = 0.5
SOFTENING = 0.25

MESH = pl.DeviceIdType.MESH
f32, bf16 = jnp.float32, jnp.bfloat16
NT = (((1,), (1,)), ((), ()))

KAPPA = WAVENUMBER / (2.0 * math.pi)
KAPPA2 = KAPPA * KAPPA
CHORD = 2.0 * RADIUS * RADIUS * KAPPA2
ROOT_CHORD = math.sqrt(CHORD)
MAGIC = 12582912.0
DARK = 2.0**127
SIN = (4.441535736857015, -7.264681196614785, 3.252051034939137)
COS = (1.4142040822010087, -6.977642112452626, 5.715238841259401, -1.728349684464805)
TURN = (
    6.283185306487509,
    -41.341701929774175,
    81.60520943123053,
    -76.70366783378654,
    41.999989934944594,
    -14.337025371611837,
)
TILE = 256
ROWS = 32
GROUPS = 6


def poly(x, coefs):
    total = coefs[-1]
    for c in coefs[-2::-1]:
        total = c + x * total
    return total


def split3(x):
    hi = x.astype(bf16).astype(f32)
    rest = x - hi
    mid = rest.astype(bf16).astype(f32)
    return hi, mid, rest - mid


def trig_rows(angle, row):
    g = angle * (0.5 / math.pi) + jnp.where(row == 3, 0.25, 0.0)
    g = jnp.where(g > 0.5, g - 1.0, g)
    h = jnp.where(g > 0.25, 0.5 - g, jnp.where(g < -0.25, -0.5 - g, g))
    return h * poly(h * h, TURN)


def target_features(axial, angle, into, d):
    width = axial.shape[1]
    row = lax.broadcasted_iota(jnp.int32, (8, width), 0)
    lane = lax.broadcasted_iota(jnp.int32, (8, width), 1)
    a = KAPPA * (axial if d == 0 else 1.0 - axial)
    q = jnp.where(row == 0, a * a, jnp.where(row == 1, a, 1.0))
    q = jnp.where(row >= 3, ROOT_CHORD * trig_rows(angle, row), q)
    block = jnp.where(lane < width // 2, 5, 6)
    q = jnp.where(row >= 5, jnp.where(row == block, 2.0, 0.0), q)
    hi, mid, low = split3(q)
    full = jnp.concatenate([hi, hi, hi, mid, mid, low], 0)
    full = jnp.concatenate([full, jnp.zeros((128 - 8 * GROUPS, width), f32)], 0)
    into[d] = full.T[:, : 8 * GROUPS].astype(bf16)


def source_features(geo, lit, into, d, patches):
    row = lax.broadcasted_iota(jnp.int32, (8, 128), 0)

    def block(jb, _):
        sl = pl.ds(pl.multiple_of(jb * 128, 128), 128)
        axial = jnp.broadcast_to(geo[d, 0, :, sl], (8, 128))
        angle = jnp.broadcast_to(geo[d, 1, :, sl], (8, 128))
        area = jnp.broadcast_to(geo[d, 2, :, sl], (8, 128))
        b = KAPPA * jnp.where(d == 0, 1.0 - axial, axial)
        bb = b * b + CHORD
        low_rows = jnp.where(row == 0, 1.0, jnp.where(row == 1, 2.0 * b, bb))
        trig = jnp.where(row >= 5, 0.0, -ROOT_CHORD * trig_rows(angle, row))
        q = jnp.where(row >= 3, trig, low_rows)
        weight = (patches / KAPPA2) / (area * area)
        soft = jnp.where(row == 2, q + SOFTENING * KAPPA2, q) * weight
        dark0 = (1 - lit[0, d, 0, jb]).astype(f32) * DARK
        dark1 = (1 - lit[0, d, 1, jb]).astype(f32) * DARK
        soft = jnp.where(row == 5, dark0, jnp.where(row == 6, dark1, soft))
        for which, value in ((0, q), (1, soft)):
            hi, mid, low = split3(value)
            into[d, which, :, sl] = jnp.concatenate([hi, mid, low, hi, mid, hi], 0).astype(bf16)
        return 0

    lax.fori_loop(0, patches // 128, block, 0, unroll=4)


def kernel_tile(q_ref, soft_ref, table, at):
    for i0 in range(0, TILE, ROWS):
        sl = pl.ds(i0, ROWS)
        q = jnp.maximum(q_ref[sl, :], 1e-30)
        m = lax.rsqrt(soft_ref[sl, :])
        t = q * lax.rsqrt(q)
        f = t - ((t + MAGIC) - MAGIC)
        ff = f * f
        s = f * poly(ff, SIN)
        c = poly(ff, COS)
        u = m * s
        table[at, sl, 0:TILE] = (m - u * s).astype(bf16)
        table[at, sl, TILE : 2 * TILE] = (u * c).astype(bf16)


def build_tables(d, tfeat, sfeat, buffers, tables, tiles):
    def distances(tile, pair):
        js = pl.ds(pl.multiple_of(tile * TILE, TILE), TILE)
        for which in (0, 1):
            pair[which][...] = jnp.dot(
                tfeat[d], sfeat[d, which, :, js], preferred_element_type=f32
            )

    distances(0, buffers[0])

    def step(k, _):
        distances(2 * k + 1, buffers[1])
        kernel_tile(*buffers[0], tables[0], d * (tiles // 2) + k)
        distances(jnp.minimum(2 * k + 2, tiles - 1), buffers[0])
        kernel_tile(*buffers[1], tables[1], d * (tiles // 2) + k)
        return 0

    lax.fori_loop(0, tiles // 2, step, 0)


def couple(d, blocks, tables, tiles, half):
    def product(tile, k, par):
        c = blocks[d, 2 * k + par]
        turned = jnp.concatenate([c[half:], -c[:half]], 0)
        both = jnp.concatenate([c, turned], 1)
        return lax.dot_general(both, tables[par][tile], NT, preferred_element_type=f32)

    def step(k, total):
        tile = d * (tiles // 2) + k
        return total + product(tile, k, 0) + product(tile, k, 1)

    return lax.fori_loop(0, tiles // 2, step, jnp.zeros((2 * half, TILE), f32), unroll=8)


def column(row_values, start, count):
    row = lax.broadcasted_iota(jnp.int32, (count, row_values.shape[1]), 0)
    lane = lax.broadcasted_iota(jnp.int32, (count, row_values.shape[1]), 1)
    wide = jnp.broadcast_to(row_values, (count, row_values.shape[1]))
    return jnp.sum(jnp.where(lane == row + start, wide, 0.0), axis=1, keepdims=True)


def reflect(coef, values, half):
    re, im = values[:half], values[half:]
    cr, ci = coef
    return jnp.concatenate([cr * re - ci * im, cr * im + ci * re], 0)


def sweep_kernel(
    segs, parts, axial_ref, angle_ref, area_ref, inc_ref, lit_ref, end_ref, out_ref,
    geo, tfeat, sfeat, q0, soft0, q1, soft1, table0, table1, cur1, cur2, state,
    geo_send, geo_recv, send_sem, recv_sem,
):
    seg, part = lax.axis_index("seg"), lax.axis_index("patch")
    patches = axial_ref.shape[1]
    tiles = patches // TILE
    half = inc_ref.shape[1] // 4
    after, before = lax.rem(seg + 1, segs), lax.rem(seg + segs - 1, segs)

    barrier = pltpu.get_barrier_semaphore()

    def greet(k, _):
        for other in (before, after):
            pl.semaphore_signal(barrier, inc=1, device_id=(other, k), device_id_type=MESH)
        return 0

    lax.fori_loop(0, parts, greet, 0)
    pl.semaphore_wait(barrier, 2 * parts)

    geo_copies = []
    for c, ref in enumerate((axial_ref, angle_ref, area_ref)):
        for d, other in ((0, after), (1, before)):
            copy = pltpu.make_async_remote_copy(
                src_ref=ref, dst_ref=geo.at[d, c],
                send_sem=geo_send.at[d, c], recv_sem=geo_recv.at[d, c],
                device_id=(other, part), device_id_type=MESH,
            )
            copy.start()
            geo_copies.append(copy)

    def send_currents(source, sweep, blocks):
        def one(k, _):
            other_part = lax.rem(part + k, parts)
            for d, other in ((0, after), (1, before)):
                pltpu.make_async_remote_copy(
                    src_ref=source.at[pl.ds(2 * half * d, 2 * half), :],
                    dst_ref=blocks.at[d, part],
                    send_sem=send_sem.at[sweep, d], recv_sem=recv_sem.at[sweep, d],
                    device_id=(other, other_part), device_id_type=MESH,
                ).start()
            return 0

        lax.fori_loop(0, parts, one, 0)

    def all_blocks(sweep, d, blocks):
        return pltpu.make_async_remote_copy(
            src_ref=blocks.at[d], dst_ref=blocks.at[d],
            send_sem=send_sem.at[sweep, d], recv_sem=recv_sem.at[sweep, d],
            device_id=(after, part), device_id_type=MESH,
        )

    send_currents(inc_ref.at[0], 0, cur1)

    at = pl.ds(pl.multiple_of(part * TILE, TILE), TILE)
    own_axial = jnp.broadcast_to(axial_ref[:, at], (8, TILE))
    own_angle = jnp.broadcast_to(angle_ref[:, at], (8, TILE))
    for d in (0, 1):
        target_features(own_axial, own_angle, tfeat, d)
    for copy in geo_copies:
        copy.wait_recv()

    tables = (table0, table1)
    for d in (0, 1):
        source_features(geo, lit_ref, sfeat, d, patches)
        build_tables(d, tfeat, sfeat, ((q0, soft0), (q1, soft1)), tables, tiles)

    first = (column(end_ref[0:1, :], 0, half), column(end_ref[0:1, :], half, half))
    last = (column(end_ref[1:2, :], 0, half), column(end_ref[1:2, :], half, half))
    incident = inc_ref[0].astype(f32)
    at_first, at_last = seg == 0, seg == segs - 1
    current = incident
    for sweep, blocks in ((0, cur1), (1, cur2)):
        for d in (0, 1):
            all_blocks(sweep, d, blocks).wait_recv()
        forward = couple(0, blocks, tables, tiles, half)
        backward = couple(1, blocks, tables, tiles, half)
        forward = jnp.where(at_first, reflect(first, current[2 * half :], half), forward)
        backward = jnp.where(at_last, reflect(last, current[: 2 * half], half), backward)
        total = (incident + jnp.concatenate([forward, backward], 0)).astype(bf16)
        if sweep == 0:
            state[...] = total
            current = total.astype(f32)
            send_currents(state, 1, cur2)
        else:
            out_ref[0] = total
    for copy in geo_copies:
        copy.wait_send()
    for sweep, blocks in ((0, cur1), (1, cur2)):
        for d in (0, 1):
            all_blocks(sweep, d, blocks).wait_send()


def on_device(segs, parts, incident, wall_axial, wall_angle, wall_area, visibility, end_reflection):
    channels, width = incident.shape[1:]
    patches = wall_axial.shape[1]
    half = channels // 4
    tiles = patches // TILE
    vmem = pl.BlockSpec(memory_space=pltpu.VMEM)
    buffer = pltpu.VMEM((TILE, TILE), f32)
    table = pltpu.VMEM((tiles, TILE, 2 * TILE), bf16)
    blocks = pltpu.VMEM((2, parts, 2 * half, width), bf16)
    return pl.pallas_call(
        functools.partial(sweep_kernel, segs, parts),
        out_shape=jax.ShapeDtypeStruct(incident.shape, bf16),
        in_specs=[vmem] * 4 + [pl.BlockSpec(memory_space=pltpu.SMEM), vmem],
        out_specs=vmem,
        scratch_shapes=[
            pltpu.VMEM((2, 3, 1, patches), f32),
            pltpu.VMEM((2, TILE, 8 * GROUPS), bf16),
            pltpu.VMEM((2, 2, 8 * GROUPS, patches), bf16),
            buffer, buffer, buffer, buffer, table, table, blocks, blocks,
            pltpu.VMEM((channels, width), bf16),
            pltpu.SemaphoreType.DMA((2, 3)),
            pltpu.SemaphoreType.DMA((2, 3)),
            pltpu.SemaphoreType.DMA((2, 2)),
            pltpu.SemaphoreType.DMA((2, 2)),
        ],
        compiler_params=pltpu.CompilerParams(
            collective_id=0, has_side_effects=True, vmem_limit_bytes=48 << 20
        ),
    )(wall_axial, wall_angle, wall_area, incident, visibility, end_reflection)


def solution(mesh):
    return jax.shard_map(
        functools.partial(on_device, mesh.shape["seg"], mesh.shape["patch"]),
        mesh=mesh,
        in_specs=(
            P("seg", None, "patch"),
            P("seg", None),
            P("seg", None),
            P("seg", None),
            P("seg", None, "patch", None),
            P(),
        ),
        out_specs=P("seg", None, "patch"),
        check_vma=False,
    )
```

```python
import functools
import math

import jax
import jax.numpy as jnp
from jax import lax
from jax.experimental import pallas as pl
from jax.experimental.pallas import tpu as pltpu
from jax.sharding import PartitionSpec as P

ITERS = 2
WAVENUMBER = 40.0
RADIUS = 0.5
SOFTENING = 0.25

MESH = pl.DeviceIdType.MESH
f32, bf16 = jnp.float32, jnp.bfloat16
NT = (((1,), (1,)), ((), ()))

KAPPA = WAVENUMBER / (2.0 * math.pi)
KAPPA2 = KAPPA * KAPPA
CHORD = 2.0 * RADIUS * RADIUS * KAPPA2
ROOT_CHORD = math.sqrt(CHORD)
MAGIC = 12582912.0
DARK = 2.0**127
SIN = (4.441535736857015, -7.264681196614785, 3.252051034939137)
COS = (1.4142040822010087, -6.977642112452626, 5.715238841259401, -1.728349684464805)
TURN = (
    6.283185306487509,
    -41.341701929774175,
    81.60520943123053,
    -76.70366783378654,
    41.999989934944594,
    -14.337025371611837,
)
TILE = 256
ROWS = 32
GROUPS = 6


def poly(x, coefs):
    total = coefs[-1]
    for c in coefs[-2::-1]:
        total = c + x * total
    return total


def split3(x):
    hi = x.astype(bf16).astype(f32)
    rest = x - hi
    mid = rest.astype(bf16).astype(f32)
    return hi, mid, rest - mid


def trig_rows(angle, row):
    g = angle * (0.5 / math.pi) + jnp.where(row == 3, 0.25, 0.0)
    g = jnp.where(g > 0.5, g - 1.0, g)
    h = jnp.where(g > 0.25, 0.5 - g, jnp.where(g < -0.25, -0.5 - g, g))
    return h * poly(h * h, TURN)


def target_features(axial, angle, into, slot, away):
    width = axial.shape[1]
    row = lax.broadcasted_iota(jnp.int32, (8, width), 0)
    lane = lax.broadcasted_iota(jnp.int32, (8, width), 1)
    a = KAPPA * (axial if not away else 1.0 - axial)
    q = jnp.where(row == 0, a * a, jnp.where(row == 1, a, 1.0))
    q = jnp.where(row >= 3, ROOT_CHORD * trig_rows(angle, row), q)
    block = jnp.where(lane < width // 2, 5, 6)
    q = jnp.where(row >= 5, jnp.where(row == block, 2.0, 0.0), q)
    hi, mid, low = split3(q)
    full = jnp.concatenate([hi, hi, hi, mid, mid, low], 0)
    full = jnp.concatenate([full, jnp.zeros((128 - 8 * GROUPS, width), f32)], 0)
    into[slot] = full.T[:, : 8 * GROUPS].astype(bf16)


def source_features(geo, slot, d, lit, into, patches):
    row = lax.broadcasted_iota(jnp.int32, (8, 128), 0)
    turned = (1 - d).astype(f32)
    sign = 1.0 - 2.0 * turned

    def block(jb, _):
        sl = pl.ds(pl.multiple_of(jb * 128, 128), 128)
        axial = jnp.broadcast_to(geo[slot, 0, :, sl], (8, 128))
        angle = jnp.broadcast_to(geo[slot, 1, :, sl], (8, 128))
        area = jnp.broadcast_to(geo[slot, 2, :, sl], (8, 128))
        b = KAPPA * (turned + sign * axial)
        bb = b * b + CHORD
        low_rows = jnp.where(row == 0, 1.0, jnp.where(row == 1, 2.0 * b, bb))
        trig = jnp.where(row >= 5, 0.0, -ROOT_CHORD * trig_rows(angle, row))
        q = jnp.where(row >= 3, trig, low_rows)
        weight = (patches / KAPPA2) / (area * area)
        soft = jnp.where(row == 2, q + SOFTENING * KAPPA2, q) * weight
        dark0 = (1 - lit[0, d, 0, jb]).astype(f32) * DARK
        dark1 = (1 - lit[0, d, 1, jb]).astype(f32) * DARK
        soft = jnp.where(row == 5, dark0, jnp.where(row == 6, dark1, soft))
        for which, value in ((0, q), (1, soft)):
            hi, mid, low = split3(value)
            into[slot, which, :, sl] = jnp.concatenate([hi, mid, low, hi, mid, hi], 0).astype(bf16)
        return 0

    lax.fori_loop(0, patches // 128, block, 0, unroll=4)


def kernel_tile(q_ref, soft_ref, table, at):
    for i0 in range(0, TILE, ROWS):
        sl = pl.ds(i0, ROWS)
        q = jnp.maximum(q_ref[sl, :], 1e-30)
        m = lax.rsqrt(soft_ref[sl, :])
        t = q * lax.rsqrt(q)
        f = t - ((t + MAGIC) - MAGIC)
        ff = f * f
        s = f * poly(ff, SIN)
        c = poly(ff, COS)
        u = m * s
        table[at, sl, 0:TILE] = (m - u * s).astype(bf16)
        table[at, sl, TILE : 2 * TILE] = (u * c).astype(bf16)


def distances(feat, sfeat, slot, tile, pair):
    js = pl.ds(pl.multiple_of(tile * TILE, TILE), TILE)
    for which in (0, 1):
        pair[which][...] = jnp.dot(feat, sfeat[slot, which, :, js], preferred_element_type=f32)


def build_tables(feat, sfeat, slot, buffers, tables, tiles, first, last):
    def step(k, _):
        distances(feat[...], sfeat, slot, 2 * k + 1, buffers[1])
        kernel_tile(*buffers[0], tables[0], slot * (tiles // 2) + k)
        distances(feat[...], sfeat, slot, jnp.minimum(2 * k + 2, tiles - 1), buffers[0])
        kernel_tile(*buffers[1], tables[1], slot * (tiles // 2) + k)
        return 0

    lax.fori_loop(first, last, step, 0)


def couple(blocks, slot, tables, tiles, half):
    def product(k, par):
        c = blocks[slot, 2 * k + par]
        turned = jnp.concatenate([c[half:], -c[:half]], 0)
        both = jnp.concatenate([c, turned], 1)
        table = tables[par][slot * (tiles // 2) + k]
        return lax.dot_general(both, table, NT, preferred_element_type=f32)

    def step(k, total):
        return total + product(k, 0) + product(k, 1)

    return lax.fori_loop(0, tiles // 2, step, jnp.zeros((2 * half, TILE), f32), unroll=8)


def column(row_values, start, count):
    row = lax.broadcasted_iota(jnp.int32, (count, row_values.shape[1]), 0)
    lane = lax.broadcasted_iota(jnp.int32, (count, row_values.shape[1]), 1)
    wide = jnp.broadcast_to(row_values, (count, row_values.shape[1]))
    return jnp.sum(jnp.where(lane == row + start, wide, 0.0), axis=1, keepdims=True)


def reflect(coef, values, half):
    re, im = values[:half], values[half:]
    cr, ci = coef
    return jnp.concatenate([cr * re - ci * im, cr * im + ci * re], 0)


NEAR, FAR = 0, 1


def sweep_kernel(
    segs, parts, axial_hbm, angle_hbm, area_hbm, inc_hbm, lit_hbm, end_hbm, out_ref,
    own, inc, end, lit, geo, tfeat, sfeat, q0, soft0, q1, soft1, table0, table1, cur1, cur2, state,
    in_sem, geo_send, geo_recv, shift_send, shift_recv, plane_send, plane_recv,
):
    seg, part = lax.axis_index("seg"), lax.axis_index("patch")
    patches = axial_hbm.shape[1]
    tiles = patches // TILE
    half = inc_hbm.shape[1] // 4
    core = lax.rem(seg, 2)
    near = seg + 1 - 2 * core
    far = seg - 1 + 2 * core
    has_far = jnp.logical_and(far >= 0, far < segs)
    d_near, d_far = 1 - core, core

    loads = [
        pltpu.make_async_copy(src, dst, in_sem.at[n])
        for n, (src, dst) in enumerate((
            (axial_hbm, own.at[0]), (angle_hbm, own.at[1]), (area_hbm, own.at[2]),
            (inc_hbm.at[0], inc), (end_hbm, end), (lit_hbm, lit),
        ))
    ]
    for load in loads:
        load.start()

    barrier = pltpu.get_barrier_semaphore()

    def greet(k, _):
        other = lax.rem(part + k, parts)
        pl.semaphore_signal(barrier, inc=1, device_id=(seg, other), device_id_type=MESH)
        return 0

    pl.semaphore_signal(barrier, inc=1, device_id=(near, part), device_id_type=MESH)

    @pl.when(has_far)
    def _():
        pl.semaphore_signal(barrier, inc=1, device_id=(far, part), device_id_type=MESH)

    lax.fori_loop(1, parts, greet, 0)

    for load in loads:
        load.wait()
    at = pl.ds(pl.multiple_of(part * TILE, TILE), TILE)
    own_axial = jnp.broadcast_to(own[0, :, at], (8, TILE))
    own_angle = jnp.broadcast_to(own[1, :, at], (8, TILE))
    for d in (0, 1):
        target_features(own_axial, own_angle, tfeat, d, d == 1)

    @pl.when(jnp.logical_not(has_far))
    def _():
        geo[FAR] = jnp.ones_like(geo[FAR])
        cur1[FAR] = jnp.zeros_like(cur1[FAR])
        cur2[FAR] = jnp.zeros_like(cur2[FAR])

    pl.semaphore_wait(barrier, parts + has_far.astype(jnp.int32))

    def geometry(slot):
        return [
            pltpu.make_async_remote_copy(
                src_ref=own.at[c], dst_ref=geo.at[slot, c],
                send_sem=geo_send.at[slot, c], recv_sem=geo_recv.at[slot, c],
                device_id=(near if slot == NEAR else far, part), device_id_type=MESH,
            )
            for c in range(3)
        ]

    def shift(source, sweep, blocks, slot):
        d = d_far if slot == NEAR else d_near
        return pltpu.make_async_remote_copy(
            src_ref=source.at[pl.ds(pl.multiple_of(2 * half * d, 2 * half), 2 * half), :],
            dst_ref=blocks.at[slot, part],
            send_sem=shift_send.at[sweep, slot], recv_sem=shift_recv.at[sweep, slot],
            device_id=(near if slot == NEAR else far, part), device_id_type=MESH,
        )

    def pass_on(sweep, blocks, slot):
        def one(k, _):
            other = lax.rem(part + k, parts)
            pltpu.make_async_remote_copy(
                src_ref=blocks.at[slot, part], dst_ref=blocks.at[slot, part],
                send_sem=plane_send.at[sweep, slot], recv_sem=plane_recv.at[sweep, slot],
                device_id=(seg, other), device_id_type=MESH,
            ).start()
            return 0

        lax.fori_loop(1, parts, one, 0)

    def plane(sweep, blocks, slot):
        most = blocks.at[slot, pl.ds(0, parts - 1)]
        return pltpu.make_async_remote_copy(
            src_ref=most, dst_ref=most,
            send_sem=plane_send.at[sweep, slot], recv_sem=plane_recv.at[sweep, slot],
            device_id=(near, part), device_id_type=MESH,
        )

    def if_far(act):
        pl.when(has_far)(act)

    near_geo, far_geo = geometry(NEAR), geometry(FAR)
    for copy in near_geo:
        copy.start()
    shift(inc, 0, cur1, NEAR).start()

    @if_far
    def _():
        shift(inc, 0, cur1, FAR).start()
        for copy in far_geo:
            copy.start()

    tables = (table0, table1)
    buffers = ((q0, soft0), (q1, soft1))
    near_feat, far_feat = tfeat.at[d_near], tfeat.at[d_far]

    shift(inc, 0, cur1, NEAR).wait_recv()
    pass_on(0, cur1, NEAR)
    for copy in near_geo:
        copy.wait_recv()
    source_features(geo, NEAR, d_near, lit, sfeat, patches)
    distances(near_feat[...], sfeat, NEAR, 0, buffers[0])
    build_tables(near_feat, sfeat, NEAR, buffers, tables, tiles, 0, tiles // 4)

    @if_far
    def _():
        shift(inc, 0, cur1, FAR).wait_recv()
        pass_on(0, cur1, FAR)

    build_tables(near_feat, sfeat, NEAR, buffers, tables, tiles, tiles // 4, tiles // 2)

    first = (column(end[0:1, :], 0, half), column(end[0:1, :], half, half))
    last = (column(end[1:2, :], 0, half), column(end[1:2, :], half, half))
    is_first = (core == 0).astype(f32)
    mirror = [is_first * f + (1.0 - is_first) * l for f, l in zip(first, last)]

    def rows(d):
        return pl.ds(pl.multiple_of(2 * half * d, 2 * half), 2 * half)

    def near_sum(blocks):
        return inc[rows(d_near), :].astype(f32) + couple(blocks, NEAR, tables, tiles, half)

    def far_sum(blocks, previous):
        coupled = couple(blocks, FAR, tables, tiles, half)
        mirrored = reflect(mirror, previous[rows(d_near), :].astype(f32), half)
        return inc[rows(d_far), :].astype(f32) + jnp.where(has_far, coupled, mirrored)

    plane(0, cur1, NEAR).wait_recv()
    state[rows(d_near), :] = near_sum(cur1).astype(bf16)

    @if_far
    def _():
        shift(state, 1, cur2, FAR).start()
        for copy in far_geo:
            copy.wait_recv()

    source_features(geo, FAR, d_far, lit, sfeat, patches)
    distances(far_feat[...], sfeat, FAR, 0, buffers[0])
    build_tables(far_feat, sfeat, FAR, buffers, tables, tiles, 0, 3 * tiles // 8)

    @if_far
    def _():
        shift(state, 1, cur2, FAR).wait_recv()
        pass_on(1, cur2, FAR)

    build_tables(far_feat, sfeat, FAR, buffers, tables, tiles, 3 * tiles // 8, tiles // 2)

    @if_far
    def _():
        plane(0, cur1, FAR).wait_recv()

    state[rows(d_far), :] = far_sum(cur1, inc).astype(bf16)
    shift(state, 1, cur2, NEAR).start()
    shift(state, 1, cur2, NEAR).wait_recv()
    pass_on(1, cur2, NEAR)

    @if_far
    def _():
        plane(1, cur2, FAR).wait_recv()

    out_ref[0, rows(d_far), :] = far_sum(cur2, state).astype(bf16)
    plane(1, cur2, NEAR).wait_recv()
    out_ref[0, rows(d_near), :] = near_sum(cur2).astype(bf16)

    for copy in near_geo:
        copy.wait_send()
    for sweep, source, blocks in ((0, inc, cur1), (1, state, cur2)):
        shift(source, sweep, blocks, NEAR).wait_send()
        plane(sweep, blocks, NEAR).wait_send()

    @if_far
    def _():
        for copy in far_geo:
            copy.wait_send()
        for sweep, source, blocks in ((0, inc, cur1), (1, state, cur2)):
            shift(source, sweep, blocks, FAR).wait_send()
            plane(sweep, blocks, FAR).wait_send()


def on_device(segs, parts, incident, wall_axial, wall_angle, wall_area, visibility, end_reflection):
    channels, width = incident.shape[1:]
    patches = wall_axial.shape[1]
    half = channels // 4
    tiles = patches // TILE
    buffer = pltpu.VMEM((TILE, TILE), f32)
    table = pltpu.VMEM((tiles, TILE, 2 * TILE), bf16)
    blocks = pltpu.VMEM((2, parts, 2 * half, width), bf16)
    rows = pltpu.VMEM((channels, width), bf16)
    return pl.pallas_call(
        functools.partial(sweep_kernel, segs, parts),
        out_shape=jax.ShapeDtypeStruct(incident.shape, bf16),
        in_specs=[pl.BlockSpec(memory_space=pl.ANY)] * 6,
        out_specs=pl.BlockSpec(memory_space=pltpu.VMEM),
        scratch_shapes=[
            pltpu.VMEM((3, 1, patches), f32),
            rows,
            pltpu.VMEM(end_reflection.shape, f32),
            pltpu.SMEM(visibility.shape, jnp.int32),
            pltpu.VMEM((2, 3, 1, patches), f32),
            pltpu.VMEM((2, TILE, 8 * GROUPS), bf16),
            pltpu.VMEM((2, 2, 8 * GROUPS, patches), bf16),
            buffer, buffer, buffer, buffer, table, table, blocks, blocks, rows,
            pltpu.SemaphoreType.DMA((6,)),
            pltpu.SemaphoreType.DMA((2, 3)),
            pltpu.SemaphoreType.DMA((2, 3)),
            pltpu.SemaphoreType.DMA((2, 2)),
            pltpu.SemaphoreType.DMA((2, 2)),
            pltpu.SemaphoreType.DMA((2, 2)),
            pltpu.SemaphoreType.DMA((2, 2)),
        ],
        compiler_params=pltpu.CompilerParams(
            collective_id=0, has_side_effects=True, vmem_limit_bytes=56 << 20
        ),
    )(wall_axial, wall_angle, wall_area, incident, visibility, end_reflection)


def solution(mesh):
    return jax.shard_map(
        functools.partial(on_device, mesh.shape["seg"], mesh.shape["patch"]),
        mesh=mesh,
        in_specs=(
            P("seg", None, "patch"),
            P("seg", None),
            P("seg", None),
            P("seg", None),
            P("seg", None, "patch", None),
            P(),
        ),
        out_specs=P("seg", None, "patch"),
        check_vma=False,
    )
```

```python
import functools
import math

import jax
import jax.numpy as jnp
from jax import lax
from jax.experimental import pallas as pl
from jax.experimental.pallas import tpu as pltpu
from jax.sharding import PartitionSpec as P

ITERS = 2
WAVENUMBER = 40.0
RADIUS = 0.5
SOFTENING = 0.25

MESH = pl.DeviceIdType.MESH
f32, bf16 = jnp.float32, jnp.bfloat16
NT = (((1,), (1,)), ((), ()))

KAPPA = WAVENUMBER / (2.0 * math.pi)
KAPPA2 = KAPPA * KAPPA
CHORD = 2.0 * RADIUS * RADIUS * KAPPA2
ROOT_CHORD = math.sqrt(CHORD)
MAGIC = 12582912.0
DARK = 2.0**127
SIN = (4.441535736857015, -7.264681196614785, 3.252051034939137)
COS = (1.4142040822010087, -6.977642112452626, 5.715238841259401, -1.728349684464805)
TURN = (
    6.283185306487509,
    -41.341701929774175,
    81.60520943123053,
    -76.70366783378654,
    41.999989934944594,
    -14.337025371611837,
)
TILE = 256
ROWS = 32
GROUPS = 6


def poly(x, coefs):
    total = coefs[-1]
    for c in coefs[-2::-1]:
        total = c + x * total
    return total


def split3(x):
    hi = x.astype(bf16).astype(f32)
    rest = x - hi
    mid = rest.astype(bf16).astype(f32)
    return hi, mid, rest - mid


def trig_rows(angle, row):
    g = angle * (0.5 / math.pi) + jnp.where(row == 3, 0.25, 0.0)
    g = jnp.where(g > 0.5, g - 1.0, g)
    h = jnp.where(g > 0.25, 0.5 - g, jnp.where(g < -0.25, -0.5 - g, g))
    return h * poly(h * h, TURN)


def target_features(axial, angle, into, slot, away):
    width = axial.shape[1]
    row = lax.broadcasted_iota(jnp.int32, (8, width), 0)
    lane = lax.broadcasted_iota(jnp.int32, (8, width), 1)
    a = KAPPA * (axial if not away else 1.0 - axial)
    q = jnp.where(row == 0, a * a, jnp.where(row == 1, a, 1.0))
    q = jnp.where(row >= 3, ROOT_CHORD * trig_rows(angle, row), q)
    block = jnp.where(lane < width // 2, 5, 6)
    q = jnp.where(row >= 5, jnp.where(row == block, 2.0, 0.0), q)
    hi, mid, low = split3(q)
    full = jnp.concatenate([hi, hi, hi, mid, mid, low], 0)
    full = jnp.concatenate([full, jnp.zeros((128 - 8 * GROUPS, width), f32)], 0)
    into[slot] = full.T[:, : 8 * GROUPS].astype(bf16)


def source_features(geo, slot, d, lit, into, patches):
    row = lax.broadcasted_iota(jnp.int32, (8, 128), 0)
    turned = (1 - d).astype(f32)
    sign = 1.0 - 2.0 * turned

    def block(jb, _):
        sl = pl.ds(pl.multiple_of(jb * 128, 128), 128)
        axial = jnp.broadcast_to(geo[slot, 0, :, sl], (8, 128))
        angle = jnp.broadcast_to(geo[slot, 1, :, sl], (8, 128))
        area = jnp.broadcast_to(geo[slot, 2, :, sl], (8, 128))
        b = KAPPA * (turned + sign * axial)
        bb = b * b + CHORD
        low_rows = jnp.where(row == 0, 1.0, jnp.where(row == 1, 2.0 * b, bb))
        trig = jnp.where(row >= 5, 0.0, -ROOT_CHORD * trig_rows(angle, row))
        q = jnp.where(row >= 3, trig, low_rows)
        weight = (patches / KAPPA2) / (area * area)
        soft = jnp.where(row == 2, q + SOFTENING * KAPPA2, q) * weight
        dark0 = (1 - lit[0, d, 0, jb]).astype(f32) * DARK
        dark1 = (1 - lit[0, d, 1, jb]).astype(f32) * DARK
        soft = jnp.where(row == 5, dark0, jnp.where(row == 6, dark1, soft))
        for which, value in ((0, q), (1, soft)):
            hi, mid, low = split3(value)
            into[slot, which, :, sl] = jnp.concatenate([hi, mid, low, hi, mid, hi], 0).astype(bf16)
        return 0

    lax.fori_loop(0, patches // 128, block, 0, unroll=4)


def kernel_tile(q_ref, soft_ref, table, at):
    for i0 in range(0, TILE, ROWS):
        sl = pl.ds(i0, ROWS)
        q = jnp.maximum(q_ref[sl, :], 1e-30)
        m = lax.rsqrt(soft_ref[sl, :])
        t = q * lax.rsqrt(q)
        f = t - ((t + MAGIC) - MAGIC)
        ff = f * f
        s = f * poly(ff, SIN)
        c = poly(ff, COS)
        u = m * s
        table[at, sl, 0:TILE] = (m - u * s).astype(bf16)
        table[at, sl, TILE : 2 * TILE] = (u * c).astype(bf16)


def distances(feat, sfeat, slot, tile, pair):
    js = pl.ds(pl.multiple_of(tile * TILE, TILE), TILE)
    for which in (0, 1):
        pair[which][...] = jnp.dot(feat, sfeat[slot, which, :, js], preferred_element_type=f32)


def build_table(feat, sfeat, slot, buffers, table, tiles, first, last, beside):
    def step(k, _):
        beside(k, 0)
        distances(feat[...], sfeat, slot, 2 * k + 1, buffers[1])
        kernel_tile(*buffers[0], table, 2 * k)
        beside(k, 1)
        distances(feat[...], sfeat, slot, jnp.minimum(2 * k + 2, tiles - 1), buffers[0])
        kernel_tile(*buffers[1], table, 2 * k + 1)
        return 0

    if first == 0:
        distances(feat[...], sfeat, slot, 0, buffers[0])
    lax.fori_loop(first, last, step, 0)


def product(block, table, half):
    turned = jnp.concatenate([block[half:], -block[:half]], 0)
    both = jnp.concatenate([block, turned], 1)
    return lax.dot_general(both, table, NT, preferred_element_type=f32)


def couple(blocks, slot, table, base, count, half):
    def step(k, total):
        return total + product(blocks[slot, base + k], table[base + k], half)

    return lax.fori_loop(0, count, step, jnp.zeros((2 * half, TILE), f32), unroll=4)


def column(row_values, start, count):
    row = lax.broadcasted_iota(jnp.int32, (count, row_values.shape[1]), 0)
    lane = lax.broadcasted_iota(jnp.int32, (count, row_values.shape[1]), 1)
    wide = jnp.broadcast_to(row_values, (count, row_values.shape[1]))
    return jnp.sum(jnp.where(lane == row + start, wide, 0.0), axis=1, keepdims=True)


def reflect(coef, values, half):
    re, im = values[:half], values[half:]
    cr, ci = coef
    return jnp.concatenate([cr * re - ci * im, cr * im + ci * re], 0)


NEAR, FAR = 0, 1


def sweep_kernel(
    segs, parts, axial_hbm, angle_hbm, area_hbm, inc_hbm, lit_hbm, end_hbm, out_ref,
    own, inc, end, lit, geo, tfeat, sfeat, q0, soft0, q1, soft1, near_table, far_table, cur1, cur2, state, total,
    in_sem, geo_send, geo_recv, sent, row_recv, side_recv,
):
    seg, part = lax.axis_index("seg"), lax.axis_index("patch")
    patches = axial_hbm.shape[1]
    tiles = patches // TILE
    half = inc_hbm.shape[1] // 4
    core = lax.rem(seg, 2)
    near = seg + 1 - 2 * core
    far = seg - 1 + 2 * core
    has_far = jnp.logical_and(far >= 0, far < segs)
    d_near, d_far = 1 - core, core

    loads = [
        pltpu.make_async_copy(src, dst, in_sem.at[n])
        for n, (src, dst) in enumerate((
            (axial_hbm, own.at[0]), (angle_hbm, own.at[1]), (area_hbm, own.at[2]),
            (inc_hbm.at[0], inc), (end_hbm, end), (lit_hbm, lit),
        ))
    ]
    for load in loads:
        load.start()

    barrier = pltpu.get_barrier_semaphore()

    ring = parts // 2
    place, side = lax.rem(part, ring), part // ring
    own_base, other_base = side * ring, (1 - side) * ring
    across = other_base + place

    def in_row(base, n):
        return base + lax.rem(place + n, ring)

    for n in range(ring):
        pl.semaphore_signal(barrier, inc=1, device_id=(near, in_row(own_base, n)), device_id_type=MESH)
    pl.semaphore_signal(barrier, inc=1, device_id=(seg, across), device_id_type=MESH)

    @pl.when(has_far)
    def _():
        for n in range(ring):
            pl.semaphore_signal(barrier, inc=1, device_id=(far, in_row(other_base, n)), device_id_type=MESH)

    @pl.when(jnp.logical_not(has_far))
    def _():
        geo[FAR] = jnp.ones_like(geo[FAR])
        cur1[FAR] = jnp.zeros_like(cur1[FAR])
        cur2[FAR] = jnp.zeros_like(cur2[FAR])

    pl.semaphore_wait(barrier, ring + 1 + ring * has_far.astype(jnp.int32))

    def geometry(slot):
        return [
            pltpu.make_async_remote_copy(
                src_ref=ref, dst_ref=geo.at[slot, c],
                send_sem=geo_send.at[slot, c], recv_sem=geo_recv.at[slot, c],
                device_id=(near, part) if slot == NEAR else (far, across), device_id_type=MESH,
            )
            for c, ref in enumerate((axial_hbm, angle_hbm, area_hbm))
        ]

    steps = [n for k in range(1, ring // 2) for n in (k, ring - k)] + [ring // 2]

    def spread(source, sweep, blocks, slot):
        d = d_far if slot == NEAR else d_near
        for n in [*steps[::-1], 0]:
            pltpu.make_async_remote_copy(
                src_ref=source.at[pl.ds(pl.multiple_of(2 * half * d, 2 * half), 2 * half), :],
                dst_ref=blocks.at[slot, part],
                send_sem=sent.at[sweep, slot], recv_sem=row_recv.at[sweep, slot, n],
                device_id=(near, in_row(own_base, n)) if slot == NEAR else (far, in_row(other_base, n)),
                device_id_type=MESH,
            ).start()

    def hand_across(sweep, blocks, slot, which):
        for n in which:
            block = blocks.at[slot, in_row(own_base if slot == NEAR else other_base, ring - n)]

            def copy(recv):
                return pltpu.make_async_remote_copy(
                    src_ref=block, dst_ref=block, send_sem=sent.at[sweep, slot], recv_sem=recv,
                    device_id=(seg, across), device_id_type=MESH,
                )

            copy(row_recv.at[sweep, slot, n]).wait_recv()
            copy(side_recv.at[sweep, slot]).start()

    def whole(sweep, blocks, slot, count):
        some = blocks.at[slot, pl.ds(0, count)]
        return pltpu.make_async_remote_copy(
            src_ref=some, dst_ref=some,
            send_sem=sent.at[sweep, slot], recv_sem=side_recv.at[sweep, slot],
            device_id=(seg, across), device_id_type=MESH,
        )

    def handed_here(sweep, blocks, slot):
        whole(sweep, blocks, slot, ring).wait_recv()

    def if_far(act):
        pl.when(has_far)(act)

    near_geo, far_geo = geometry(NEAR), geometry(FAR)
    for copy in near_geo:
        copy.start()
    spread(inc_hbm.at[0], 0, cur1, NEAR)

    @if_far
    def _():
        for copy in far_geo:
            copy.start()
        spread(inc_hbm.at[0], 0, cur1, FAR)

    for load in loads:
        load.wait()
    at = pl.ds(pl.multiple_of(part * TILE, TILE), TILE)
    own_axial = jnp.broadcast_to(own[0, :, at], (8, TILE))
    own_angle = jnp.broadcast_to(own[1, :, at], (8, TILE))
    for d in (0, 1):
        target_features(own_axial, own_angle, tfeat, d, d == 1)

    buffers = ((q0, soft0), (q1, soft1))
    near_feat, far_feat = tfeat.at[d_near], tfeat.at[d_far]
    early, late = [0, *steps[:4]], steps[4:]
    pairs = tiles // 2

    for copy in near_geo:
        copy.wait_recv()
    source_features(geo, NEAR, d_near, lit, sfeat, patches)

    def beside_near(k, part_of):
        if part_of:
            return

        @pl.when(k == pairs // 2)
        def _():
            hand_across(0, cur1, NEAR, early)

    build_table(near_feat, sfeat, NEAR, buffers, near_table, tiles, 0, pairs, beside_near)
    hand_across(0, cur1, NEAR, late)

    first = (column(end[0:1, :], 0, half), column(end[0:1, :], half, half))
    last = (column(end[1:2, :], 0, half), column(end[1:2, :], half, half))
    is_first = (core == 0).astype(f32)
    mirror = [is_first * f + (1.0 - is_first) * l for f, l in zip(first, last)]

    @if_far
    def _():
        for copy in far_geo:
            copy.wait_recv()

    source_features(geo, FAR, d_far, lit, sfeat, patches)
    total[...] = jnp.zeros_like(total)

    def beside_far(k, part_of):
        if part_of == 0:

            @pl.when(jnp.logical_and(has_far, k == 1))
            def _():
                hand_across(0, cur1, FAR, early)

            @pl.when(k == pairs // 4)
            def _():
                handed_here(0, cur1, NEAR)

        tile = jnp.where(k < pairs // 4, own_base, other_base - ring) + 4 * k + 2 * part_of
        for n in (0, 1):
            total[...] += product(cur1[NEAR, tile + n], near_table[tile + n], half)

    build_table(far_feat, sfeat, FAR, buffers, far_table, tiles, 0, pairs // 2, beside_far)

    def rows(d):
        return pl.ds(pl.multiple_of(2 * half * d, 2 * half), 2 * half)

    state[rows(d_near), :] = (inc[rows(d_near), :].astype(f32) + total[...]).astype(bf16)

    @if_far
    def _():
        spread(state, 1, cur2, FAR)
        hand_across(0, cur1, FAR, late)

    build_table(far_feat, sfeat, FAR, buffers, far_table, tiles, pairs // 2, pairs, lambda k, part_of: None)

    def far_result(coupled, previous):
        mirrored = reflect(mirror, previous[rows(d_near), :].astype(f32), half)
        return (inc[rows(d_far), :].astype(f32) + jnp.where(has_far, coupled, mirrored)).astype(bf16)

    coupled = couple(cur1, FAR, far_table, other_base, ring, half)

    @if_far
    def _():
        handed_here(0, cur1, FAR)

    coupled += couple(cur1, FAR, far_table, own_base, ring, half)
    state[rows(d_far), :] = far_result(coupled, inc)
    spread(state, 1, cur2, NEAR)

    @if_far
    def _():
        hand_across(1, cur2, FAR, early)

    hand_across(1, cur2, NEAR, early)

    @if_far
    def _():
        hand_across(1, cur2, FAR, late)

    hand_across(1, cur2, NEAR, late)

    near_coupled = couple(cur2, NEAR, near_table, own_base, ring, half)
    far_coupled = couple(cur2, FAR, far_table, other_base, ring, half)
    handed_here(1, cur2, NEAR)
    near_coupled += couple(cur2, NEAR, near_table, other_base, ring, half)
    out_ref[0, rows(d_near), :] = (inc[rows(d_near), :].astype(f32) + near_coupled).astype(bf16)

    @if_far
    def _():
        handed_here(1, cur2, FAR)

    far_coupled += couple(cur2, FAR, far_table, own_base, ring, half)
    out_ref[0, rows(d_far), :] = far_result(far_coupled, state)

    for copy in near_geo:
        copy.wait_send()
    for sweep, blocks in ((0, cur1), (1, cur2)):
        whole(sweep, blocks, NEAR, parts).wait_send()

    @if_far
    def _():
        for copy in far_geo:
            copy.wait_send()
        for sweep, blocks in ((0, cur1), (1, cur2)):
            whole(sweep, blocks, FAR, parts).wait_send()


def on_device(segs, parts, incident, wall_axial, wall_angle, wall_area, visibility, end_reflection):
    channels, width = incident.shape[1:]
    patches = wall_axial.shape[1]
    half = channels // 4
    tiles = patches // TILE
    buffer = pltpu.VMEM((TILE, TILE), f32)
    table = pltpu.VMEM((tiles, TILE, 2 * TILE), bf16)
    blocks = pltpu.VMEM((2, parts, 2 * half, width), bf16)
    rows = pltpu.VMEM((channels, width), bf16)
    return pl.pallas_call(
        functools.partial(sweep_kernel, segs, parts),
        out_shape=jax.ShapeDtypeStruct(incident.shape, bf16),
        in_specs=[pl.BlockSpec(memory_space=pl.ANY)] * 6,
        out_specs=pl.BlockSpec(memory_space=pltpu.VMEM),
        scratch_shapes=[
            pltpu.VMEM((3, 1, patches), f32),
            rows,
            pltpu.VMEM(end_reflection.shape, f32),
            pltpu.SMEM(visibility.shape, jnp.int32),
            pltpu.VMEM((2, 3, 1, patches), f32),
            pltpu.VMEM((2, TILE, 8 * GROUPS), bf16),
            pltpu.VMEM((2, 2, 8 * GROUPS, patches), bf16),
            buffer, buffer, buffer, buffer, table, table, blocks, blocks, rows,
            pltpu.VMEM((2 * half, width), f32),
            pltpu.SemaphoreType.DMA((6,)),
            pltpu.SemaphoreType.DMA((2, 3)),
            pltpu.SemaphoreType.DMA((2, 3)),
            pltpu.SemaphoreType.DMA((2, 2)),
            pltpu.SemaphoreType.DMA((2, 2, parts // 2)),
            pltpu.SemaphoreType.DMA((2, 2)),
        ],
        compiler_params=pltpu.CompilerParams(
            collective_id=0, has_side_effects=True, vmem_limit_bytes=56 << 20
        ),
    )(wall_axial, wall_angle, wall_area, incident, visibility, end_reflection)


def solution(mesh):
    return jax.shard_map(
        functools.partial(on_device, mesh.shape["seg"], mesh.shape["patch"]),
        mesh=mesh,
        in_specs=(
            P("seg", None, "patch"),
            P("seg", None),
            P("seg", None),
            P("seg", None),
            P("seg", None, "patch", None),
            P(),
        ),
        out_specs=P("seg", None, "patch"),
        check_vma=False,
    )
```

```python
import functools
import math

import jax
import jax.numpy as jnp
from jax import lax
from jax.experimental import pallas as pl
from jax.experimental.pallas import tpu as pltpu
from jax.sharding import PartitionSpec as P

ITERS = 2
WAVENUMBER = 40.0
RADIUS = 0.5
SOFTENING = 0.25

MESH = pl.DeviceIdType.MESH
f32, bf16 = jnp.float32, jnp.bfloat16
NT = (((1,), (1,)), ((), ()))

KAPPA = WAVENUMBER / (2.0 * math.pi)
KAPPA2 = KAPPA * KAPPA
CHORD = 2.0 * RADIUS * RADIUS * KAPPA2
ROOT_CHORD = math.sqrt(CHORD)
MAGIC = 12582912.0
DARK = 2.0**127
SIN = (4.441535736857015, -7.264681196614785, 3.252051034939137)
COS = (1.4142040822010087, -6.977642112452626, 5.715238841259401, -1.728349684464805)
TURN = (
    6.283185306487509,
    -41.341701929774175,
    81.60520943123053,
    -76.70366783378654,
    41.999989934944594,
    -14.337025371611837,
)
TILE = 256
ROWS = 32
GROUPS = 6


def poly(x, coefs):
    total = coefs[-1]
    for c in coefs[-2::-1]:
        total = c + x * total
    return total


def split3(x):
    hi = x.astype(bf16).astype(f32)
    rest = x - hi
    mid = rest.astype(bf16).astype(f32)
    return hi, mid, rest - mid


def trig_rows(angle, row):
    g = angle * (0.5 / math.pi) + jnp.where(row == 3, 0.25, 0.0)
    g = jnp.where(g > 0.5, g - 1.0, g)
    h = jnp.where(g > 0.25, 0.5 - g, jnp.where(g < -0.25, -0.5 - g, g))
    return h * poly(h * h, TURN)


def target_features(axial, angle, into, slot, away):
    width = axial.shape[1]
    row = lax.broadcasted_iota(jnp.int32, (8, width), 0)
    lane = lax.broadcasted_iota(jnp.int32, (8, width), 1)
    a = KAPPA * (axial if not away else 1.0 - axial)
    q = jnp.where(row == 0, a * a, jnp.where(row == 1, a, 1.0))
    q = jnp.where(row >= 3, ROOT_CHORD * trig_rows(angle, row), q)
    block = jnp.where(lane < width // 2, 5, 6)
    q = jnp.where(row >= 5, jnp.where(row == block, 2.0, 0.0), q)
    hi, mid, low = split3(q)
    full = jnp.concatenate([hi, hi, hi, mid, mid, low], 0)
    full = jnp.concatenate([full, jnp.zeros((128 - 8 * GROUPS, width), f32)], 0)
    into[slot] = full.T[:, : 8 * GROUPS].astype(bf16)


def source_features(geo, slot, d, lit, into, patches):
    row = lax.broadcasted_iota(jnp.int32, (8, 128), 0)
    turned = (1 - d).astype(f32)
    sign = 1.0 - 2.0 * turned

    def block(jb, _):
        sl = pl.ds(pl.multiple_of(jb * 128, 128), 128)
        axial = jnp.broadcast_to(geo[slot, 0, :, sl], (8, 128))
        angle = jnp.broadcast_to(geo[slot, 1, :, sl], (8, 128))
        area = jnp.broadcast_to(geo[slot, 2, :, sl], (8, 128))
        b = KAPPA * (turned + sign * axial)
        bb = b * b + CHORD
        low_rows = jnp.where(row == 0, 1.0, jnp.where(row == 1, 2.0 * b, bb))
        trig = jnp.where(row >= 5, 0.0, -ROOT_CHORD * trig_rows(angle, row))
        q = jnp.where(row >= 3, trig, low_rows)
        weight = (patches / KAPPA2) / (area * area)
        soft = jnp.where(row == 2, q + SOFTENING * KAPPA2, q) * weight
        dark0 = (1 - lit[0, d, 0, jb]).astype(f32) * DARK
        dark1 = (1 - lit[0, d, 1, jb]).astype(f32) * DARK
        soft = jnp.where(row == 5, dark0, jnp.where(row == 6, dark1, soft))
        for which, value in ((0, q), (1, soft)):
            hi, mid, low = split3(value)
            into[slot, which, :, sl] = jnp.concatenate([hi, mid, low, hi, mid, hi], 0).astype(bf16)
        return 0

    lax.fori_loop(0, patches // 128, block, 0, unroll=4)


def kernel_tile(q_ref, soft_ref, table, at):
    for i0 in range(0, TILE, ROWS):
        sl = pl.ds(i0, ROWS)
        q = jnp.maximum(q_ref[sl, :], 1e-30)
        m = lax.rsqrt(soft_ref[sl, :])
        t = q * lax.rsqrt(q)
        f = t - ((t + MAGIC) - MAGIC)
        ff = f * f
        s = f * poly(ff, SIN)
        c = poly(ff, COS)
        u = m * s
        table[at, sl, 0:TILE] = (m - u * s).astype(bf16)
        table[at, sl, TILE : 2 * TILE] = (u * c).astype(bf16)


def distances(feat, sfeat, slot, tile, pair):
    js = pl.ds(pl.multiple_of(tile * TILE, TILE), TILE)
    for which in (0, 1):
        pair[which][...] = jnp.dot(feat, sfeat[slot, which, :, js], preferred_element_type=f32)


def build_table(feat, sfeat, slot, buffers, table, tiles, first, last, beside):
    def step(k, _):
        beside(k, 0)
        distances(feat[...], sfeat, slot, 2 * k + 1, buffers[1])
        kernel_tile(*buffers[0], table, 2 * k)
        beside(k, 1)
        distances(feat[...], sfeat, slot, jnp.minimum(2 * k + 2, tiles - 1), buffers[0])
        kernel_tile(*buffers[1], table, 2 * k + 1)
        return 0

    if first == 0:
        distances(feat[...], sfeat, slot, 0, buffers[0])
    lax.fori_loop(first, last, step, 0)


def product(block, table, half):
    turned = jnp.concatenate([block[half:], -block[:half]], 0)
    both = jnp.concatenate([block, turned], 1)
    return lax.dot_general(both, table, NT, preferred_element_type=f32)


def couple(blocks, slot, table, base, count, half):
    def step(k, total):
        return total + product(blocks[slot, base + k], table[base + k], half)

    return lax.fori_loop(0, count, step, jnp.zeros((2 * half, TILE), f32), unroll=4)


def column(row_values, start, count):
    row = lax.broadcasted_iota(jnp.int32, (count, row_values.shape[1]), 0)
    lane = lax.broadcasted_iota(jnp.int32, (count, row_values.shape[1]), 1)
    wide = jnp.broadcast_to(row_values, (count, row_values.shape[1]))
    return jnp.sum(jnp.where(lane == row + start, wide, 0.0), axis=1, keepdims=True)


def reflect(coef, values, half):
    re, im = values[:half], values[half:]
    cr, ci = coef
    return jnp.concatenate([cr * re - ci * im, cr * im + ci * re], 0)


NEAR, FAR = 0, 1


def sweep_kernel(
    segs, parts, axial_hbm, angle_hbm, area_hbm, inc_hbm, lit_hbm, end_hbm, out_ref,
    own, inc, end, lit, geo, tfeat, sfeat, q0, soft0, q1, soft1, near_table, far_table, cur1, cur2, state, total,
    in_sem, geo_send, geo_recv, sent, row_recv, side_recv,
):
    seg, part = lax.axis_index("seg"), lax.axis_index("patch")
    patches = axial_hbm.shape[1]
    tiles = patches // TILE
    half = inc_hbm.shape[1] // 4
    core = lax.rem(seg, 2)
    near = seg + 1 - 2 * core
    far = seg - 1 + 2 * core
    has_far = jnp.logical_and(far >= 0, far < segs)
    d_near, d_far = 1 - core, core

    loads = [
        pltpu.make_async_copy(src, dst, in_sem.at[n])
        for n, (src, dst) in enumerate((
            (axial_hbm, own.at[0]), (angle_hbm, own.at[1]), (area_hbm, own.at[2]),
            (inc_hbm.at[0], inc), (end_hbm, end), (lit_hbm, lit),
        ))
    ]
    for load in loads:
        load.start()

    barrier = pltpu.get_barrier_semaphore()

    ring = parts // 2
    place, side = lax.rem(part, ring), part // ring
    own_base, other_base = side * ring, (1 - side) * ring
    across = other_base + place

    def in_row(base, n):
        return base + lax.rem(place + n, ring)

    for n in range(ring):
        pl.semaphore_signal(barrier, inc=1, device_id=(near, in_row(own_base, n)), device_id_type=MESH)
    pl.semaphore_signal(barrier, inc=1, device_id=(seg, across), device_id_type=MESH)

    @pl.when(has_far)
    def _():
        for n in range(ring):
            pl.semaphore_signal(barrier, inc=1, device_id=(far, in_row(other_base, n)), device_id_type=MESH)

    @pl.when(jnp.logical_not(has_far))
    def _():
        geo[FAR] = jnp.ones_like(geo[FAR])
        cur1[FAR] = jnp.zeros_like(cur1[FAR])
        cur2[FAR] = jnp.zeros_like(cur2[FAR])

    pl.semaphore_wait(barrier, ring + 1 + ring * has_far.astype(jnp.int32))

    def geometry(slot):
        return [
            pltpu.make_async_remote_copy(
                src_ref=ref, dst_ref=geo.at[slot, c],
                send_sem=geo_send.at[slot, c], recv_sem=geo_recv.at[slot, c],
                device_id=(near, part) if slot == NEAR else (far, across), device_id_type=MESH,
            )
            for c, ref in enumerate((axial_hbm, angle_hbm, area_hbm))
        ]

    def spread_one(source, sweep, blocks, slot, n):
        d = d_far if slot == NEAR else d_near
        pltpu.make_async_remote_copy(
            src_ref=source.at[pl.ds(pl.multiple_of(2 * half * d, 2 * half), 2 * half), :],
            dst_ref=blocks.at[slot, part],
            send_sem=sent.at[sweep, slot], recv_sem=row_recv.at[sweep, slot, place],
            device_id=(near, in_row(own_base, n)) if slot == NEAR else (far, in_row(other_base, n)),
            device_id_type=MESH,
        ).start()

    def spread(source, sweep, blocks, slot):
        for n in [k for m in range(ring // 2, 0, -1) for k in sorted({m, ring - m})] + [0]:
            spread_one(source, sweep, blocks, slot, n)

    quad = ring // 2
    own_quad = place // quad

    def hand_across(sweep, blocks, slot, later):
        start = quad * (1 - own_quad if later else own_quad)
        base = (own_base if slot == NEAR else other_base) + start

        def copy(ref, recv):
            return pltpu.make_async_remote_copy(
                src_ref=ref, dst_ref=ref, send_sem=sent.at[sweep, slot], recv_sem=recv,
                device_id=(seg, across), device_id_type=MESH,
            )

        for n in range(quad):
            copy(blocks.at[slot, base + n], row_recv.at[sweep, slot, start + n]).wait_recv()
        copy(blocks.at[slot, pl.ds(base, quad)], side_recv.at[sweep, slot]).start()

    def whole(sweep, blocks, slot, count):
        some = blocks.at[slot, pl.ds(0, count)]
        return pltpu.make_async_remote_copy(
            src_ref=some, dst_ref=some,
            send_sem=sent.at[sweep, slot], recv_sem=side_recv.at[sweep, slot],
            device_id=(seg, across), device_id_type=MESH,
        )

    def handed_here(sweep, blocks, slot):
        whole(sweep, blocks, slot, ring).wait_recv()

    def if_far(act):
        pl.when(has_far)(act)

    near_geo, far_geo = geometry(NEAR), geometry(FAR)
    for copy in near_geo:
        copy.start()
    spread(inc_hbm.at[0], 0, cur1, NEAR)

    @if_far
    def _():
        for copy in far_geo:
            copy.start()

    for load in loads:
        load.wait()
    at = pl.ds(pl.multiple_of(part * TILE, TILE), TILE)
    own_axial = jnp.broadcast_to(own[0, :, at], (8, TILE))
    own_angle = jnp.broadcast_to(own[1, :, at], (8, TILE))
    for d in (0, 1):
        target_features(own_axial, own_angle, tfeat, d, d == 1)

    buffers = ((q0, soft0), (q1, soft1))
    near_feat, far_feat = tfeat.at[d_near], tfeat.at[d_far]
    pairs = tiles // 2

    for copy in near_geo:
        copy.wait_recv()
    source_features(geo, NEAR, d_near, lit, sfeat, patches)

    def beside_near(k, part_of):
        @pl.when(jnp.logical_and(has_far, k < ring // 2))
        def _():
            spread_one(inc_hbm.at[0], 0, cur1, FAR, ring // 2 + 2 * k + part_of)

        if part_of == 0:

            @pl.when(k == 4)
            def _():
                hand_across(0, cur1, NEAR, False)

            @pl.when(k == 6)
            def _():
                hand_across(0, cur1, NEAR, True)

    build_table(near_feat, sfeat, NEAR, buffers, near_table, tiles, 0, pairs, beside_near)

    first = (column(end[0:1, :], 0, half), column(end[0:1, :], half, half))
    last = (column(end[1:2, :], 0, half), column(end[1:2, :], half, half))
    is_first = (core == 0).astype(f32)
    mirror = [is_first * f + (1.0 - is_first) * l for f, l in zip(first, last)]

    @if_far
    def _():
        for copy in far_geo:
            copy.wait_recv()

    source_features(geo, FAR, d_far, lit, sfeat, patches)
    total[...] = jnp.zeros_like(total)

    def beside_far(k, part_of):
        if part_of == 0:

            @pl.when(jnp.logical_and(has_far, k == 1))
            def _():
                hand_across(0, cur1, FAR, False)

            @pl.when(k == pairs // 4)
            def _():
                handed_here(0, cur1, NEAR)

        tile = jnp.where(k < pairs // 4, own_base, other_base - ring) + 4 * k + 2 * part_of
        for n in (0, 1):
            total[...] += product(cur1[NEAR, tile + n], near_table[tile + n], half)

    build_table(far_feat, sfeat, FAR, buffers, far_table, tiles, 0, pairs // 2, beside_far)

    def rows(d):
        return pl.ds(pl.multiple_of(2 * half * d, 2 * half), 2 * half)

    state[rows(d_near), :] = (inc[rows(d_near), :].astype(f32) + total[...]).astype(bf16)

    @if_far
    def _():
        hand_across(0, cur1, FAR, True)

    def beside_rest(k, part_of):
        @if_far
        def _():
            spread_one(state, 1, cur2, FAR, ring // 2 + 2 * (k - pairs // 2) + part_of)

    build_table(far_feat, sfeat, FAR, buffers, far_table, tiles, pairs // 2, pairs, beside_rest)

    def far_result(coupled, previous):
        mirrored = reflect(mirror, previous[rows(d_near), :].astype(f32), half)
        return (inc[rows(d_far), :].astype(f32) + jnp.where(has_far, coupled, mirrored)).astype(bf16)

    coupled = couple(cur1, FAR, far_table, other_base, ring, half)

    @if_far
    def _():
        handed_here(0, cur1, FAR)

    coupled += couple(cur1, FAR, far_table, own_base, ring, half)
    state[rows(d_far), :] = far_result(coupled, inc)
    spread(state, 1, cur2, NEAR)

    @if_far
    def _():
        hand_across(1, cur2, FAR, False)

    hand_across(1, cur2, NEAR, False)

    @if_far
    def _():
        hand_across(1, cur2, FAR, True)

    hand_across(1, cur2, NEAR, True)

    near_coupled = couple(cur2, NEAR, near_table, own_base, ring, half)
    far_coupled = couple(cur2, FAR, far_table, other_base, ring, half)
    handed_here(1, cur2, NEAR)
    near_coupled += couple(cur2, NEAR, near_table, other_base, ring, half)
    out_ref[0, rows(d_near), :] = (inc[rows(d_near), :].astype(f32) + near_coupled).astype(bf16)

    @if_far
    def _():
        handed_here(1, cur2, FAR)

    far_coupled += couple(cur2, FAR, far_table, own_base, ring, half)
    out_ref[0, rows(d_far), :] = far_result(far_coupled, state)

    for copy in near_geo:
        copy.wait_send()
    for sweep, blocks in ((0, cur1), (1, cur2)):
        whole(sweep, blocks, NEAR, parts).wait_send()

    @if_far
    def _():
        for copy in far_geo:
            copy.wait_send()
        for sweep, blocks in ((0, cur1), (1, cur2)):
            whole(sweep, blocks, FAR, parts).wait_send()


def on_device(segs, parts, incident, wall_axial, wall_angle, wall_area, visibility, end_reflection):
    channels, width = incident.shape[1:]
    patches = wall_axial.shape[1]
    half = channels // 4
    tiles = patches // TILE
    buffer = pltpu.VMEM((TILE, TILE), f32)
    table = pltpu.VMEM((tiles, TILE, 2 * TILE), bf16)
    blocks = pltpu.VMEM((2, parts, 2 * half, width), bf16)
    rows = pltpu.VMEM((channels, width), bf16)
    return pl.pallas_call(
        functools.partial(sweep_kernel, segs, parts),
        out_shape=jax.ShapeDtypeStruct(incident.shape, bf16),
        in_specs=[pl.BlockSpec(memory_space=pl.ANY)] * 6,
        out_specs=pl.BlockSpec(memory_space=pltpu.VMEM),
        scratch_shapes=[
            pltpu.VMEM((3, 1, patches), f32),
            rows,
            pltpu.VMEM(end_reflection.shape, f32),
            pltpu.SMEM(visibility.shape, jnp.int32),
            pltpu.VMEM((2, 3, 1, patches), f32),
            pltpu.VMEM((2, TILE, 8 * GROUPS), bf16),
            pltpu.VMEM((2, 2, 8 * GROUPS, patches), bf16),
            buffer, buffer, buffer, buffer, table, table, blocks, blocks, rows,
            pltpu.VMEM((2 * half, width), f32),
            pltpu.SemaphoreType.DMA((6,)),
            pltpu.SemaphoreType.DMA((2, 3)),
            pltpu.SemaphoreType.DMA((2, 3)),
            pltpu.SemaphoreType.DMA((2, 2)),
            pltpu.SemaphoreType.DMA((2, 2, parts // 2)),
            pltpu.SemaphoreType.DMA((2, 2)),
        ],
        compiler_params=pltpu.CompilerParams(
            collective_id=0, has_side_effects=True, vmem_limit_bytes=56 << 20
        ),
    )(wall_axial, wall_angle, wall_area, incident, visibility, end_reflection)


def solution(mesh):
    return jax.shard_map(
        functools.partial(on_device, mesh.shape["seg"], mesh.shape["patch"]),
        mesh=mesh,
        in_specs=(
            P("seg", None, "patch"),
            P("seg", None),
            P("seg", None),
            P("seg", None),
            P("seg", None, "patch", None),
            P(),
        ),
        out_specs=P("seg", None, "patch"),
        check_vma=False,
    )
```

```python
import functools
import math

import jax
import jax.numpy as jnp
from jax import lax
from jax.experimental import pallas as pl
from jax.experimental.pallas import tpu as pltpu
from jax.sharding import PartitionSpec as P

ITERS = 2
WAVENUMBER = 40.0
RADIUS = 0.5
SOFTENING = 0.25

MESH = pl.DeviceIdType.MESH
f32, bf16 = jnp.float32, jnp.bfloat16
NT = (((1,), (1,)), ((), ()))

KAPPA = WAVENUMBER / (2.0 * math.pi)
KAPPA2 = KAPPA * KAPPA
CHORD = 2.0 * RADIUS * RADIUS * KAPPA2
ROOT_CHORD = math.sqrt(CHORD)
MAGIC = 12582912.0
DARK = 2.0**127
SIN = (4.441535736857015, -7.264681196614785, 3.252051034939137)
COS = (1.4142040822010087, -6.977642112452626, 5.715238841259401, -1.728349684464805)
TURN = (
    6.283185306487509,
    -41.341701929774175,
    81.60520943123053,
    -76.70366783378654,
    41.999989934944594,
    -14.337025371611837,
)
TILE = 256
ROWS = 32
GROUPS = 6


def poly(x, coefs):
    total = coefs[-1]
    for c in coefs[-2::-1]:
        total = c + x * total
    return total


def split3(x):
    hi = x.astype(bf16).astype(f32)
    rest = x - hi
    mid = rest.astype(bf16).astype(f32)
    return hi, mid, rest - mid


def trig_rows(angle, row):
    g = angle * (0.5 / math.pi) + jnp.where(row == 3, 0.25, 0.0)
    g = jnp.where(g > 0.5, g - 1.0, g)
    h = jnp.where(g > 0.25, 0.5 - g, jnp.where(g < -0.25, -0.5 - g, g))
    return h * poly(h * h, TURN)


def target_features(axial, angle, into, slot, away):
    width = axial.shape[1]
    row = lax.broadcasted_iota(jnp.int32, (8, width), 0)
    lane = lax.broadcasted_iota(jnp.int32, (8, width), 1)
    a = KAPPA * (axial if not away else 1.0 - axial)
    q = jnp.where(row == 0, a * a, jnp.where(row == 1, a, 1.0))
    q = jnp.where(row >= 3, ROOT_CHORD * trig_rows(angle, row), q)
    block = jnp.where(lane < width // 2, 5, 6)
    q = jnp.where(row >= 5, jnp.where(row == block, 2.0, 0.0), q)
    hi, mid, low = split3(q)
    full = jnp.concatenate([hi, hi, hi, mid, mid, low], 0)
    full = jnp.concatenate([full, jnp.zeros((128 - 8 * GROUPS, width), f32)], 0)
    into[slot] = full.T[:, : 8 * GROUPS].astype(bf16)


def source_features(geo, slot, d, lit, into, patches):
    row = lax.broadcasted_iota(jnp.int32, (8, 128), 0)
    turned = (1 - d).astype(f32)
    sign = 1.0 - 2.0 * turned

    def block(jb, _):
        sl = pl.ds(pl.multiple_of(jb * 128, 128), 128)
        axial = jnp.broadcast_to(geo[slot, 0, :, sl], (8, 128))
        angle = jnp.broadcast_to(geo[slot, 1, :, sl], (8, 128))
        area = jnp.broadcast_to(geo[slot, 2, :, sl], (8, 128))
        b = KAPPA * (turned + sign * axial)
        bb = b * b + CHORD
        low_rows = jnp.where(row == 0, 1.0, jnp.where(row == 1, 2.0 * b, bb))
        trig = jnp.where(row >= 5, 0.0, -ROOT_CHORD * trig_rows(angle, row))
        q = jnp.where(row >= 3, trig, low_rows)
        weight = (patches / KAPPA2) / (area * area)
        soft = jnp.where(row == 2, q + SOFTENING * KAPPA2, q) * weight
        dark0 = (1 - lit[0, d, 0, jb]).astype(f32) * DARK
        dark1 = (1 - lit[0, d, 1, jb]).astype(f32) * DARK
        soft = jnp.where(row == 5, dark0, jnp.where(row == 6, dark1, soft))
        for which, value in ((0, q), (1, soft)):
            hi, mid, low = split3(value)
            into[slot, which, :, sl] = jnp.concatenate([hi, mid, low, hi, mid, hi], 0).astype(bf16)
        return 0

    lax.fori_loop(0, patches // 128, block, 0, unroll=4)


def kernel_tile(q_ref, soft_ref, table, at):
    for i0 in range(0, TILE, ROWS):
        sl = pl.ds(i0, ROWS)
        q = jnp.maximum(q_ref[sl, :], 1e-30)
        m = lax.rsqrt(soft_ref[sl, :])
        t = q * lax.rsqrt(q)
        f = t - ((t + MAGIC) - MAGIC)
        ff = f * f
        s = f * poly(ff, SIN)
        c = poly(ff, COS)
        u = m * s
        table[at, sl, 0:TILE] = (m - u * s).astype(bf16)
        table[at, sl, TILE : 2 * TILE] = (u * c).astype(bf16)


def distances(feat, sfeat, slot, tile, pair):
    js = pl.ds(pl.multiple_of(tile * TILE, TILE), TILE)
    for which in (0, 1):
        pair[which][...] = jnp.dot(feat, sfeat[slot, which, :, js], preferred_element_type=f32)


def build_table(feat, sfeat, slot, buffers, table, tiles, first, last, beside):
    def step(k, _):
        beside(k, 0)
        distances(feat[...], sfeat, slot, 2 * k + 1, buffers[1])
        kernel_tile(*buffers[0], table, 2 * k)
        beside(k, 1)
        distances(feat[...], sfeat, slot, jnp.minimum(2 * k + 2, tiles - 1), buffers[0])
        kernel_tile(*buffers[1], table, 2 * k + 1)
        return 0

    if first == 0:
        distances(feat[...], sfeat, slot, 0, buffers[0])
    lax.fori_loop(first, last, step, 0)


def product(block, table, half):
    turned = jnp.concatenate([block[half:], -block[:half]], 0)
    both = jnp.concatenate([block, turned], 1)
    return lax.dot_general(both, table, NT, preferred_element_type=f32)


def couple(blocks, slot, table, base, count, half):
    def step(k, total):
        return total + product(blocks[slot, base + k], table[base + k], half)

    return lax.fori_loop(0, count, step, jnp.zeros((2 * half, TILE), f32), unroll=4)


def column(row_values, start, count):
    row = lax.broadcasted_iota(jnp.int32, (count, row_values.shape[1]), 0)
    lane = lax.broadcasted_iota(jnp.int32, (count, row_values.shape[1]), 1)
    wide = jnp.broadcast_to(row_values, (count, row_values.shape[1]))
    return jnp.sum(jnp.where(lane == row + start, wide, 0.0), axis=1, keepdims=True)


def reflect(coef, values, half):
    re, im = values[:half], values[half:]
    cr, ci = coef
    return jnp.concatenate([cr * re - ci * im, cr * im + ci * re], 0)


NEAR, FAR = 0, 1


def sweep_kernel(
    segs, parts, axial_hbm, angle_hbm, area_hbm, inc_hbm, lit_hbm, end_hbm, out_ref,
    own, inc, end, lit, geo, tfeat, sfeat, q0, soft0, q1, soft1, near_table, far_table, cur1, cur2, state, total,
    in_sem, geo_send, geo_recv, sent, row_recv, side_recv,
):
    seg, part = lax.axis_index("seg"), lax.axis_index("patch")
    patches = axial_hbm.shape[1]
    tiles = patches // TILE
    half = inc_hbm.shape[1] // 4
    core = lax.rem(seg, 2)
    near = seg + 1 - 2 * core
    far = seg - 1 + 2 * core
    has_far = jnp.logical_and(far >= 0, far < segs)
    d_near, d_far = 1 - core, core

    loads = [
        pltpu.make_async_copy(src, dst, in_sem.at[n])
        for n, (src, dst) in enumerate((
            (axial_hbm, own.at[0]), (angle_hbm, own.at[1]), (area_hbm, own.at[2]),
            (inc_hbm.at[0], inc), (end_hbm, end), (lit_hbm, lit),
        ))
    ]
    for load in loads:
        load.start()

    barrier = pltpu.get_barrier_semaphore()

    ring = parts // 2
    place, side = lax.rem(part, ring), part // ring
    own_base, other_base = side * ring, (1 - side) * ring
    across = other_base + place

    def in_row(base, n):
        return base + lax.rem(place + n, ring)

    for n in range(ring):
        pl.semaphore_signal(barrier, inc=1, device_id=(near, in_row(own_base, n)), device_id_type=MESH)
    pl.semaphore_signal(barrier, inc=1, device_id=(seg, across), device_id_type=MESH)

    @pl.when(has_far)
    def _():
        for n in range(ring):
            pl.semaphore_signal(barrier, inc=1, device_id=(far, in_row(other_base, n)), device_id_type=MESH)

    @pl.when(jnp.logical_not(has_far))
    def _():
        geo[FAR] = jnp.ones_like(geo[FAR])
        cur1[FAR] = jnp.zeros_like(cur1[FAR])
        cur2[FAR] = jnp.zeros_like(cur2[FAR])

    pl.semaphore_wait(barrier, ring + 1 + ring * has_far.astype(jnp.int32))

    def geometry(slot):
        return [
            pltpu.make_async_remote_copy(
                src_ref=ref, dst_ref=geo.at[slot, c],
                send_sem=geo_send.at[slot, c], recv_sem=geo_recv.at[slot, c],
                device_id=(near, part) if slot == NEAR else (far, across), device_id_type=MESH,
            )
            for c, ref in enumerate((axial_hbm, angle_hbm, area_hbm))
        ]

    def spread_one(source, sweep, blocks, slot, n):
        d = d_far if slot == NEAR else d_near
        pltpu.make_async_remote_copy(
            src_ref=source.at[pl.ds(pl.multiple_of(2 * half * d, 2 * half), 2 * half), :],
            dst_ref=blocks.at[slot, part],
            send_sem=sent.at[sweep, slot], recv_sem=row_recv.at[sweep, slot, place],
            device_id=(near, in_row(own_base, n)) if slot == NEAR else (far, in_row(other_base, n)),
            device_id_type=MESH,
        ).start()

    def spread(source, sweep, blocks, slot):
        for n in [k for m in range(ring // 2, 0, -1) for k in sorted({m, ring - m})] + [0]:
            spread_one(source, sweep, blocks, slot, n)

    quad = ring // 2
    own_quad = place // quad

    def hand_across(sweep, blocks, slot, later):
        start = quad * (1 - own_quad if later else own_quad)
        base = (own_base if slot == NEAR else other_base) + start

        def copy(ref, recv):
            return pltpu.make_async_remote_copy(
                src_ref=ref, dst_ref=ref, send_sem=sent.at[sweep, slot], recv_sem=recv,
                device_id=(seg, across), device_id_type=MESH,
            )

        for n in range(quad):
            copy(blocks.at[slot, base + n], row_recv.at[sweep, slot, start + n]).wait_recv()
        copy(blocks.at[slot, pl.ds(base, quad)], side_recv.at[sweep, slot, int(later)]).start()

    def whole(sweep, blocks, slot, count, later=False):
        some = blocks.at[slot, pl.ds(0, count)]
        return pltpu.make_async_remote_copy(
            src_ref=some, dst_ref=some,
            send_sem=sent.at[sweep, slot], recv_sem=side_recv.at[sweep, slot, int(later)],
            device_id=(seg, across), device_id_type=MESH,
        )

    def handed_here(sweep, blocks, slot, later):
        whole(sweep, blocks, slot, quad, later).wait_recv()

    def half_row(base, later):
        return base + quad * (1 - own_quad if later else own_quad)

    def if_far(act):
        pl.when(has_far)(act)

    near_geo, far_geo = geometry(NEAR), geometry(FAR)
    for copy in near_geo:
        copy.start()
    spread(inc_hbm.at[0], 0, cur1, NEAR)

    @if_far
    def _():
        for copy in far_geo:
            copy.start()

    for load in loads:
        load.wait()
    at = pl.ds(pl.multiple_of(part * TILE, TILE), TILE)
    own_axial = jnp.broadcast_to(own[0, :, at], (8, TILE))
    own_angle = jnp.broadcast_to(own[1, :, at], (8, TILE))
    for d in (0, 1):
        target_features(own_axial, own_angle, tfeat, d, d == 1)

    buffers = ((q0, soft0), (q1, soft1))
    near_feat, far_feat = tfeat.at[d_near], tfeat.at[d_far]
    pairs = tiles // 2

    for copy in near_geo:
        copy.wait_recv()
    source_features(geo, NEAR, d_near, lit, sfeat, patches)

    def beside_near(k, part_of):
        @pl.when(jnp.logical_and(has_far, k < ring // 2))
        def _():
            spread_one(inc_hbm.at[0], 0, cur1, FAR, ring // 2 + 2 * k + part_of)

        if part_of == 0:

            @pl.when(k == 4)
            def _():
                hand_across(0, cur1, NEAR, False)

            @pl.when(k == 6)
            def _():
                hand_across(0, cur1, NEAR, True)

    build_table(near_feat, sfeat, NEAR, buffers, near_table, tiles, 0, pairs, beside_near)

    first = (column(end[0:1, :], 0, half), column(end[0:1, :], half, half))
    last = (column(end[1:2, :], 0, half), column(end[1:2, :], half, half))
    is_first = (core == 0).astype(f32)
    mirror = [is_first * f + (1.0 - is_first) * l for f, l in zip(first, last)]

    @if_far
    def _():
        for copy in far_geo:
            copy.wait_recv()

    source_features(geo, FAR, d_far, lit, sfeat, patches)
    total[...] = jnp.zeros_like(total)

    def beside_far(k, part_of):
        if part_of == 0:

            @pl.when(jnp.logical_and(has_far, k == 1))
            def _():
                hand_across(0, cur1, FAR, False)

            @pl.when(k == pairs // 4)
            def _():
                handed_here(0, cur1, NEAR, False)
                handed_here(0, cur1, NEAR, True)

        tile = jnp.where(k < pairs // 4, own_base, other_base - ring) + 4 * k + 2 * part_of
        for n in (0, 1):
            total[...] += product(cur1[NEAR, tile + n], near_table[tile + n], half)

    build_table(far_feat, sfeat, FAR, buffers, far_table, tiles, 0, pairs // 2, beside_far)

    def rows(d):
        return pl.ds(pl.multiple_of(2 * half * d, 2 * half), 2 * half)

    state[rows(d_near), :] = (inc[rows(d_near), :].astype(f32) + total[...]).astype(bf16)

    @if_far
    def _():
        hand_across(0, cur1, FAR, True)

    def beside_rest(k, part_of):
        @if_far
        def _():
            spread_one(state, 1, cur2, FAR, ring // 2 + 2 * (k - pairs // 2) + part_of)

    build_table(far_feat, sfeat, FAR, buffers, far_table, tiles, pairs // 2, pairs, beside_rest)

    def far_result(coupled, previous):
        mirrored = reflect(mirror, previous[rows(d_near), :].astype(f32), half)
        return (inc[rows(d_far), :].astype(f32) + jnp.where(has_far, coupled, mirrored)).astype(bf16)

    coupled = couple(cur1, FAR, far_table, other_base, ring, half)

    @if_far
    def _():
        handed_here(0, cur1, FAR, False)
        handed_here(0, cur1, FAR, True)

    coupled += couple(cur1, FAR, far_table, own_base, ring, half)
    state[rows(d_far), :] = far_result(coupled, inc)
    spread(state, 1, cur2, NEAR)

    @if_far
    def _():
        hand_across(1, cur2, FAR, False)
        hand_across(1, cur2, FAR, True)

    far_coupled = couple(cur2, FAR, far_table, other_base, ring, half)
    hand_across(1, cur2, NEAR, False)
    hand_across(1, cur2, NEAR, True)
    near_coupled = couple(cur2, NEAR, near_table, own_base, ring, half)

    @if_far
    def _():
        handed_here(1, cur2, FAR, False)
        handed_here(1, cur2, FAR, True)

    far_coupled += couple(cur2, FAR, far_table, own_base, ring, half)
    out_ref[0, rows(d_far), :] = far_result(far_coupled, state)
    for later in (False, True):
        handed_here(1, cur2, NEAR, later)
        near_coupled += couple(cur2, NEAR, near_table, half_row(other_base, later), quad, half)
    out_ref[0, rows(d_near), :] = (inc[rows(d_near), :].astype(f32) + near_coupled).astype(bf16)

    for copy in near_geo:
        copy.wait_send()
    for sweep, blocks in ((0, cur1), (1, cur2)):
        whole(sweep, blocks, NEAR, parts).wait_send()

    @if_far
    def _():
        for copy in far_geo:
            copy.wait_send()
        for sweep, blocks in ((0, cur1), (1, cur2)):
            whole(sweep, blocks, FAR, parts).wait_send()


def on_device(segs, parts, incident, wall_axial, wall_angle, wall_area, visibility, end_reflection):
    channels, width = incident.shape[1:]
    patches = wall_axial.shape[1]
    half = channels // 4
    tiles = patches // TILE
    buffer = pltpu.VMEM((TILE, TILE), f32)
    table = pltpu.VMEM((tiles, TILE, 2 * TILE), bf16)
    blocks = pltpu.VMEM((2, parts, 2 * half, width), bf16)
    rows = pltpu.VMEM((channels, width), bf16)
    return pl.pallas_call(
        functools.partial(sweep_kernel, segs, parts),
        out_shape=jax.ShapeDtypeStruct(incident.shape, bf16),
        in_specs=[pl.BlockSpec(memory_space=pl.ANY)] * 6,
        out_specs=pl.BlockSpec(memory_space=pltpu.VMEM),
        scratch_shapes=[
            pltpu.VMEM((3, 1, patches), f32),
            rows,
            pltpu.VMEM(end_reflection.shape, f32),
            pltpu.SMEM(visibility.shape, jnp.int32),
            pltpu.VMEM((2, 3, 1, patches), f32),
            pltpu.VMEM((2, TILE, 8 * GROUPS), bf16),
            pltpu.VMEM((2, 2, 8 * GROUPS, patches), bf16),
            buffer, buffer, buffer, buffer, table, table, blocks, blocks, rows,
            pltpu.VMEM((2 * half, width), f32),
            pltpu.SemaphoreType.DMA((6,)),
            pltpu.SemaphoreType.DMA((2, 3)),
            pltpu.SemaphoreType.DMA((2, 3)),
            pltpu.SemaphoreType.DMA((2, 2)),
            pltpu.SemaphoreType.DMA((2, 2, parts // 2)),
            pltpu.SemaphoreType.DMA((2, 2, 2)),
        ],
        compiler_params=pltpu.CompilerParams(
            collective_id=0, has_side_effects=True, vmem_limit_bytes=56 << 20
        ),
    )(wall_axial, wall_angle, wall_area, incident, visibility, end_reflection)


def solution(mesh):
    return jax.shard_map(
        functools.partial(on_device, mesh.shape["seg"], mesh.shape["patch"]),
        mesh=mesh,
        in_specs=(
            P("seg", None, "patch"),
            P("seg", None),
            P("seg", None),
            P("seg", None),
            P("seg", None, "patch", None),
            P(),
        ),
        out_specs=P("seg", None, "patch"),
        check_vma=False,
    )
```

```python
import functools
import math

import jax
import jax.numpy as jnp
from jax import lax
from jax.experimental import pallas as pl
from jax.experimental.pallas import tpu as pltpu
from jax.sharding import PartitionSpec as P

ITERS = 2
WAVENUMBER = 40.0
RADIUS = 0.5
SOFTENING = 0.25

MESH = pl.DeviceIdType.MESH
f32, bf16 = jnp.float32, jnp.bfloat16
NT = (((1,), (1,)), ((), ()))

KAPPA = WAVENUMBER / (2.0 * math.pi)
KAPPA2 = KAPPA * KAPPA
CHORD = 2.0 * RADIUS * RADIUS * KAPPA2
ROOT_CHORD = math.sqrt(CHORD)
MAGIC = 12582912.0
DARK = 2.0**127
SIN = (4.441535736857015, -7.264681196614785, 3.252051034939137)
COS = (1.4142040822010087, -6.977642112452626, 5.715238841259401, -1.728349684464805)
TURN = (
    6.283185306487509,
    -41.341701929774175,
    81.60520943123053,
    -76.70366783378654,
    41.999989934944594,
    -14.337025371611837,
)
TILE = 256
ROWS = 32
GROUPS = 6


def poly(x, coefs):
    total = coefs[-1]
    for c in coefs[-2::-1]:
        total = c + x * total
    return total


def split3(x):
    hi = x.astype(bf16).astype(f32)
    rest = x - hi
    mid = rest.astype(bf16).astype(f32)
    return hi, mid, rest - mid


def trig_rows(angle, row):
    g = angle * (0.5 / math.pi) + jnp.where(row == 3, 0.25, 0.0)
    g = jnp.where(g > 0.5, g - 1.0, g)
    h = jnp.where(g > 0.25, 0.5 - g, jnp.where(g < -0.25, -0.5 - g, g))
    return h * poly(h * h, TURN)


def target_features(axial, angle, into, slot, away):
    width = axial.shape[1]
    row = lax.broadcasted_iota(jnp.int32, (8, width), 0)
    lane = lax.broadcasted_iota(jnp.int32, (8, width), 1)
    a = KAPPA * (axial if not away else 1.0 - axial)
    q = jnp.where(row == 0, a * a, jnp.where(row == 1, a, 1.0))
    q = jnp.where(row >= 3, ROOT_CHORD * trig_rows(angle, row), q)
    block = jnp.where(lane < width // 2, 5, 6)
    q = jnp.where(row >= 5, jnp.where(row == block, 2.0, 0.0), q)
    hi, mid, low = split3(q)
    full = jnp.concatenate([hi, hi, hi, mid, mid, low], 0)
    full = jnp.concatenate([full, jnp.zeros((128 - 8 * GROUPS, width), f32)], 0)
    into[slot] = full.T[:, : 8 * GROUPS].astype(bf16)


def source_features(geo, slot, d, lit, into, patches):
    row = lax.broadcasted_iota(jnp.int32, (8, 128), 0)
    turned = (1 - d).astype(f32)
    sign = 1.0 - 2.0 * turned

    def block(jb, _):
        sl = pl.ds(pl.multiple_of(jb * 128, 128), 128)
        axial = jnp.broadcast_to(geo[slot, 0, :, sl], (8, 128))
        angle = jnp.broadcast_to(geo[slot, 1, :, sl], (8, 128))
        area = jnp.broadcast_to(geo[slot, 2, :, sl], (8, 128))
        b = KAPPA * (turned + sign * axial)
        bb = b * b + CHORD
        low_rows = jnp.where(row == 0, 1.0, jnp.where(row == 1, 2.0 * b, bb))
        trig = jnp.where(row >= 5, 0.0, -ROOT_CHORD * trig_rows(angle, row))
        q = jnp.where(row >= 3, trig, low_rows)
        weight = (patches / KAPPA2) / (area * area)
        soft = jnp.where(row == 2, q + SOFTENING * KAPPA2, q) * weight
        dark0 = (1 - lit[0, d, 0, jb]).astype(f32) * DARK
        dark1 = (1 - lit[0, d, 1, jb]).astype(f32) * DARK
        soft = jnp.where(row == 5, dark0, jnp.where(row == 6, dark1, soft))
        for which, value in ((0, q), (1, soft)):
            hi, mid, low = split3(value)
            into[slot, which, :, sl] = jnp.concatenate([hi, mid, low, hi, mid, hi], 0).astype(bf16)
        return 0

    lax.fori_loop(0, patches // 128, block, 0, unroll=4)


def kernel_tile(q_ref, soft_ref, table, at):
    for i0 in range(0, TILE, ROWS):
        sl = pl.ds(i0, ROWS)
        q = jnp.maximum(q_ref[sl, :], 1e-30)
        m = lax.rsqrt(soft_ref[sl, :])
        t = q * lax.rsqrt(q)
        f = t - ((t + MAGIC) - MAGIC)
        ff = f * f
        s = f * poly(ff, SIN)
        c = poly(ff, COS)
        u = m * s
        table[at, sl, 0:TILE] = (m - u * s).astype(bf16)
        table[at, sl, TILE : 2 * TILE] = (u * c).astype(bf16)


def distances(feat, sfeat, slot, tile, pair):
    js = pl.ds(pl.multiple_of(tile * TILE, TILE), TILE)
    for which in (0, 1):
        pair[which][...] = jnp.dot(feat, sfeat[slot, which, :, js], preferred_element_type=f32)


def build_table(feat, sfeat, slot, buffers, table, tiles, first, last, beside):
    def step(k, _):
        beside(k, 0)
        distances(feat[...], sfeat, slot, 2 * k + 1, buffers[1])
        kernel_tile(*buffers[0], table, 2 * k)
        beside(k, 1)
        distances(feat[...], sfeat, slot, jnp.minimum(2 * k + 2, tiles - 1), buffers[0])
        kernel_tile(*buffers[1], table, 2 * k + 1)
        return 0

    if first == 0:
        distances(feat[...], sfeat, slot, 0, buffers[0])
    lax.fori_loop(first, last, step, 0)


def product(block, table, half):
    turned = jnp.concatenate([block[half:], -block[:half]], 0)
    both = jnp.concatenate([block, turned], 1)
    return lax.dot_general(both, table, NT, preferred_element_type=f32)


def couple(blocks, slot, table, base, count, half):
    def step(k, total):
        return total + product(blocks[slot, base + k], table[base + k], half)

    return lax.fori_loop(0, count, step, jnp.zeros((2 * half, TILE), f32), unroll=4)


def column(row_values, start, count):
    row = lax.broadcasted_iota(jnp.int32, (count, row_values.shape[1]), 0)
    lane = lax.broadcasted_iota(jnp.int32, (count, row_values.shape[1]), 1)
    wide = jnp.broadcast_to(row_values, (count, row_values.shape[1]))
    return jnp.sum(jnp.where(lane == row + start, wide, 0.0), axis=1, keepdims=True)


def reflect(coef, values, half):
    re, im = values[:half], values[half:]
    cr, ci = coef
    return jnp.concatenate([cr * re - ci * im, cr * im + ci * re], 0)


NEAR, FAR = 0, 1


def sweep_kernel(
    segs, parts, axial_hbm, angle_hbm, area_hbm, inc_hbm, lit_hbm, end_hbm, out_ref,
    own, inc, end, lit, geo, tfeat, sfeat, q0, soft0, q1, soft1, near_table, far_table, cur1, cur2, state, total,
    in_sem, geo_send, geo_recv, sent, row_recv, side_recv,
):
    seg, part = lax.axis_index("seg"), lax.axis_index("patch")
    patches = axial_hbm.shape[1]
    tiles = patches // TILE
    half = inc_hbm.shape[1] // 4
    core = lax.rem(seg, 2)
    near = seg + 1 - 2 * core
    far = seg - 1 + 2 * core
    has_far = jnp.logical_and(far >= 0, far < segs)
    d_near, d_far = 1 - core, core

    loads = [
        pltpu.make_async_copy(src, dst, in_sem.at[n])
        for n, (src, dst) in enumerate((
            (axial_hbm, own.at[0]), (angle_hbm, own.at[1]), (area_hbm, own.at[2]),
            (inc_hbm.at[0], inc), (end_hbm, end), (lit_hbm, lit),
        ))
    ]
    for load in loads:
        load.start()

    barrier = pltpu.get_barrier_semaphore()

    ring = parts // 2
    place, side = lax.rem(part, ring), part // ring
    own_base, other_base = side * ring, (1 - side) * ring
    across = other_base + place

    def in_row(base, n):
        return base + lax.rem(place + n, ring)

    for n in range(ring):
        pl.semaphore_signal(barrier, inc=1, device_id=(near, in_row(own_base, n)), device_id_type=MESH)
    pl.semaphore_signal(barrier, inc=1, device_id=(seg, across), device_id_type=MESH)

    @pl.when(has_far)
    def _():
        for n in range(ring):
            pl.semaphore_signal(barrier, inc=1, device_id=(far, in_row(other_base, n)), device_id_type=MESH)

    @pl.when(jnp.logical_not(has_far))
    def _():
        geo[FAR] = jnp.ones_like(geo[FAR])
        cur1[FAR] = jnp.zeros_like(cur1[FAR])
        cur2[FAR] = jnp.zeros_like(cur2[FAR])

    pl.semaphore_wait(barrier, ring + 1 + ring * has_far.astype(jnp.int32))

    def geometry(slot):
        return [
            pltpu.make_async_remote_copy(
                src_ref=ref, dst_ref=geo.at[slot, c],
                send_sem=geo_send.at[slot, c], recv_sem=geo_recv.at[slot, c],
                device_id=(near, part) if slot == NEAR else (far, across), device_id_type=MESH,
            )
            for c, ref in enumerate((axial_hbm, angle_hbm, area_hbm))
        ]

    def spread_one(source, sweep, blocks, slot, n):
        d = d_far if slot == NEAR else d_near
        pltpu.make_async_remote_copy(
            src_ref=source.at[pl.ds(pl.multiple_of(2 * half * d, 2 * half), 2 * half), :],
            dst_ref=blocks.at[slot, part],
            send_sem=sent.at[sweep, slot], recv_sem=row_recv.at[sweep, slot, place],
            device_id=(near, in_row(own_base, n)) if slot == NEAR else (far, in_row(other_base, n)),
            device_id_type=MESH,
        ).start()

    def spread(source, sweep, blocks, slot):
        for n in [k for m in range(ring // 2, 0, -1) for k in sorted({m, ring - m})] + [0]:
            spread_one(source, sweep, blocks, slot, n)

    quad = ring // 2
    own_quad = place // quad

    def hand_across(sweep, blocks, slot, later):
        start = quad * (1 - own_quad if later else own_quad)
        base = (own_base if slot == NEAR else other_base) + start

        def copy(ref, recv):
            return pltpu.make_async_remote_copy(
                src_ref=ref, dst_ref=ref, send_sem=sent.at[sweep, slot], recv_sem=recv,
                device_id=(seg, across), device_id_type=MESH,
            )

        count = 1 if sweep == 1 else quad
        for n in range(quad):
            copy(blocks.at[slot, base + n], row_recv.at[sweep, slot, start + n]).wait_recv()
            if (n + 1) % count == 0:
                some = blocks.at[slot, pl.ds(base + n + 1 - count, count)]
                copy(some, side_recv.at[sweep, slot, int(later)]).start()

    def whole(sweep, blocks, slot, count, later=False):
        some = blocks.at[slot, pl.ds(0, count)]
        return pltpu.make_async_remote_copy(
            src_ref=some, dst_ref=some,
            send_sem=sent.at[sweep, slot], recv_sem=side_recv.at[sweep, slot, int(later)],
            device_id=(seg, across), device_id_type=MESH,
        )

    def handed_here(sweep, blocks, slot, later):
        whole(sweep, blocks, slot, quad, later).wait_recv()

    def half_row(base, later):
        return base + quad * (1 - own_quad if later else own_quad)

    def if_far(act):
        pl.when(has_far)(act)

    near_geo, far_geo = geometry(NEAR), geometry(FAR)
    for copy in near_geo:
        copy.start()
    spread(inc_hbm.at[0], 0, cur1, NEAR)

    @if_far
    def _():
        for copy in far_geo:
            copy.start()

    for load in loads:
        load.wait()
    at = pl.ds(pl.multiple_of(part * TILE, TILE), TILE)
    own_axial = jnp.broadcast_to(own[0, :, at], (8, TILE))
    own_angle = jnp.broadcast_to(own[1, :, at], (8, TILE))
    for d in (0, 1):
        target_features(own_axial, own_angle, tfeat, d, d == 1)

    buffers = ((q0, soft0), (q1, soft1))
    near_feat, far_feat = tfeat.at[d_near], tfeat.at[d_far]
    pairs = tiles // 2

    for copy in near_geo:
        copy.wait_recv()
    source_features(geo, NEAR, d_near, lit, sfeat, patches)

    def beside_near(k, part_of):
        @pl.when(jnp.logical_and(has_far, k < ring // 2))
        def _():
            spread_one(inc_hbm.at[0], 0, cur1, FAR, ring // 2 + 2 * k + part_of)

        if part_of == 0:

            @pl.when(k == 4)
            def _():
                hand_across(0, cur1, NEAR, False)

            @pl.when(k == 6)
            def _():
                hand_across(0, cur1, NEAR, True)

    build_table(near_feat, sfeat, NEAR, buffers, near_table, tiles, 0, pairs, beside_near)

    first = (column(end[0:1, :], 0, half), column(end[0:1, :], half, half))
    last = (column(end[1:2, :], 0, half), column(end[1:2, :], half, half))
    is_first = (core == 0).astype(f32)
    mirror = [is_first * f + (1.0 - is_first) * l for f, l in zip(first, last)]

    @if_far
    def _():
        for copy in far_geo:
            copy.wait_recv()

    source_features(geo, FAR, d_far, lit, sfeat, patches)
    total[...] = jnp.zeros_like(total)

    def beside_far(k, part_of):
        if part_of == 0:

            @pl.when(jnp.logical_and(has_far, k == 1))
            def _():
                hand_across(0, cur1, FAR, False)

            @pl.when(k == pairs // 4)
            def _():
                handed_here(0, cur1, NEAR, False)
                handed_here(0, cur1, NEAR, True)

        tile = jnp.where(k < pairs // 4, own_base, other_base - ring) + 4 * k + 2 * part_of
        for n in (0, 1):
            total[...] += product(cur1[NEAR, tile + n], near_table[tile + n], half)

    build_table(far_feat, sfeat, FAR, buffers, far_table, tiles, 0, pairs // 2, beside_far)

    def rows(d):
        return pl.ds(pl.multiple_of(2 * half * d, 2 * half), 2 * half)

    state[rows(d_near), :] = (inc[rows(d_near), :].astype(f32) + total[...]).astype(bf16)

    @if_far
    def _():
        hand_across(0, cur1, FAR, True)

    def beside_rest(k, part_of):
        @if_far
        def _():
            spread_one(state, 1, cur2, FAR, ring // 2 + 2 * (k - pairs // 2) + part_of)

    build_table(far_feat, sfeat, FAR, buffers, far_table, tiles, pairs // 2, pairs, beside_rest)

    def far_result(coupled, previous):
        mirrored = reflect(mirror, previous[rows(d_near), :].astype(f32), half)
        return (inc[rows(d_far), :].astype(f32) + jnp.where(has_far, coupled, mirrored)).astype(bf16)

    coupled = couple(cur1, FAR, far_table, other_base, ring, half)

    @if_far
    def _():
        handed_here(0, cur1, FAR, False)
        handed_here(0, cur1, FAR, True)

    coupled += couple(cur1, FAR, far_table, own_base, ring, half)
    state[rows(d_far), :] = far_result(coupled, inc)
    spread(state, 1, cur2, NEAR)

    @if_far
    def _():
        hand_across(1, cur2, FAR, False)
        hand_across(1, cur2, FAR, True)

    far_coupled = couple(cur2, FAR, far_table, other_base, ring, half)
    hand_across(1, cur2, NEAR, False)
    hand_across(1, cur2, NEAR, True)
    near_coupled = couple(cur2, NEAR, near_table, own_base, ring, half)

    @if_far
    def _():
        handed_here(1, cur2, FAR, False)
        handed_here(1, cur2, FAR, True)

    far_coupled += couple(cur2, FAR, far_table, own_base, ring, half)
    out_ref[0, rows(d_far), :] = far_result(far_coupled, state)
    for later in (False, True):
        handed_here(1, cur2, NEAR, later)
        near_coupled += couple(cur2, NEAR, near_table, half_row(other_base, later), quad, half)
    out_ref[0, rows(d_near), :] = (inc[rows(d_near), :].astype(f32) + near_coupled).astype(bf16)

    for copy in near_geo:
        copy.wait_send()
    for sweep, blocks in ((0, cur1), (1, cur2)):
        whole(sweep, blocks, NEAR, parts).wait_send()

    @if_far
    def _():
        for copy in far_geo:
            copy.wait_send()
        for sweep, blocks in ((0, cur1), (1, cur2)):
            whole(sweep, blocks, FAR, parts).wait_send()


def on_device(segs, parts, incident, wall_axial, wall_angle, wall_area, visibility, end_reflection):
    channels, width = incident.shape[1:]
    patches = wall_axial.shape[1]
    half = channels // 4
    tiles = patches // TILE
    buffer = pltpu.VMEM((TILE, TILE), f32)
    table = pltpu.VMEM((tiles, TILE, 2 * TILE), bf16)
    blocks = pltpu.VMEM((2, parts, 2 * half, width), bf16)
    rows = pltpu.VMEM((channels, width), bf16)
    return pl.pallas_call(
        functools.partial(sweep_kernel, segs, parts),
        out_shape=jax.ShapeDtypeStruct(incident.shape, bf16),
        in_specs=[pl.BlockSpec(memory_space=pl.ANY)] * 6,
        out_specs=pl.BlockSpec(memory_space=pltpu.VMEM),
        scratch_shapes=[
            pltpu.VMEM((3, 1, patches), f32),
            rows,
            pltpu.VMEM(end_reflection.shape, f32),
            pltpu.SMEM(visibility.shape, jnp.int32),
            pltpu.VMEM((2, 3, 1, patches), f32),
            pltpu.VMEM((2, TILE, 8 * GROUPS), bf16),
            pltpu.VMEM((2, 2, 8 * GROUPS, patches), bf16),
            buffer, buffer, buffer, buffer, table, table, blocks, blocks, rows,
            pltpu.VMEM((2 * half, width), f32),
            pltpu.SemaphoreType.DMA((6,)),
            pltpu.SemaphoreType.DMA((2, 3)),
            pltpu.SemaphoreType.DMA((2, 3)),
            pltpu.SemaphoreType.DMA((2, 2)),
            pltpu.SemaphoreType.DMA((2, 2, parts // 2)),
            pltpu.SemaphoreType.DMA((2, 2, 2)),
        ],
        compiler_params=pltpu.CompilerParams(
            collective_id=0, has_side_effects=True, vmem_limit_bytes=56 << 20
        ),
    )(wall_axial, wall_angle, wall_area, incident, visibility, end_reflection)


def solution(mesh):
    return jax.shard_map(
        functools.partial(on_device, mesh.shape["seg"], mesh.shape["patch"]),
        mesh=mesh,
        in_specs=(
            P("seg", None, "patch"),
            P("seg", None),
            P("seg", None),
            P("seg", None),
            P("seg", None, "patch", None),
            P(),
        ),
        out_specs=P("seg", None, "patch"),
        check_vma=False,
    )
```
